32 devices in a mesh: survey: 2 (over y), band: 4 (over z), role: 4 (over x, core).
Axes of the slice: x: 2, y: 2, z: 4, core: 2. Of those that a mesh axis runs over, the one named last changes fastest.
Arguments:
- vel_index: int32 [16, 32, 128], P('role', 'band'), may hold values from 0 to 31
- courant: float32 [32], replicated, may hold values from 0.05 to 0.19
- src_now: float32 [32, 32, 128], P(('survey', 'role'), 'band'), parts along dimension 0, may hold values from -4 to 4
- src_prev: float32 [32, 32, 128], P(('survey', 'role'), 'band'), parts along dimension 0, may hold values from -4 to 4
- rec_now: float32 [32, 32, 128], P(('survey', 'role'), 'band'), parts along dimension 0, may hold values from -4 to 4
- rec_prev: float32 [32, 32, 128], P(('survey', 'role'), 'band'), parts along dimension 0, may hold values from -4 to 4
- src_pos: int32 [8, 3], P('survey'), parts along dimension 0, may hold values from 0 to 127, as said below
- src_wavelet: float32 [8, 16], P('survey'), parts along dimension 0, may hold values from -16 to 16
- rec_pos: int32 [8192, 2], P('survey'), parts along dimension 0, may hold values from 0 to 127, as said below
- rec_traces: float32 [8192, 16], P('survey'), parts along dimension 0, may hold values from -16 to 16
- offset_lags: int32 [32], replicated, may hold values from -16 to 16, as said below
Outputs:
- image: bfloat16 [64, 16, 32, 128], P('survey', 'role', 'band'), parts along dimension 0
- src_final: float32 [32, 32, 128], P(('survey', 'role'), 'band'), parts along dimension 0
- rec_final: float32 [32, 32, 128], P(('survey', 'role'), 'band'), parts along dimension 0
The draws below stay inside these ranges and needn't reach their ends.
There are 2 independent parts, one for each index of `survey`. The reference program is written for one: setup_inputs(seed, part) draws one part's arguments, and reference() takes and returns one part's arrays. A program takes and returns all parts, laid end to end along the dimension named above; an argument that names none is the same for every part. Nothing has to cross between parts.
Inputs may be any that keep to these rules, and one draw needn't show every extreme that they name: `src_pos`: column 0 is a depth cell below 16, column 1 a cross-line cell below 32, column 2 an inline cell below 128; sources may share cells. `rec_pos`: column 0 is a cross-line cell below 32, column 1 an inline cell below 128; receivers may share cells. `offset_lags`: increasing and distinct: every whole number from -16 to 16 except one of the interior ones.
All inputs are finite; a program needn't handle non-finite values.
Results may differ from the reference program's by a relative error of at most 0.004.
Values may be sent and summed in bfloat16 or wider, within the bound.
A program may use at most 128 MiB of HBM per device.

```python
import jax
import jax.numpy as jnp
from jax import lax

NLAG = 32
LEVELS = 32
SUB = 4
IMAGES = 4
NSRC = 4
NREC = 4096
STEPS = 16
NZ = 16
NY = 32
NX = 128


def draw_positions(key, row_count, limits, forced):
    columns = []
    for column, upper in enumerate(limits):
        columns.append(jax.random.randint(jax.random.fold_in(key, column), (row_count,), 0, upper))
    coords = jnp.stack(columns, axis=1).astype(jnp.int32)
    for row_at, column, set_value in forced:
        coords = coords.at[row_at, column].set(set_value)
    return coords


def draw_src_pos(key, part):
    return draw_positions(jax.random.fold_in(key, 11), NSRC, (NZ, NY, NX), ((0, 2, NX - 1), (1, 1, NY - 1), (2, 0, NZ - 1)))


def draw_rec_pos(key, part):
    return draw_positions(jax.random.fold_in(key, 12), NREC, (NY, NX), ((0, 1, NX - 1), (1, 0, NY - 1)))


def draw_offset_lags(key, part):
    half_span = NLAG // 2
    missing = jax.random.randint(jax.random.fold_in(key, 13), (), 1 - half_span, half_span)
    ordered = jnp.arange(NLAG, dtype=jnp.int32) - half_span
    return (ordered + (ordered >= missing).astype(jnp.int32)).astype(jnp.int32)


def place_ends(entries, key, least, top_value):
    index_at = [jax.random.randint(jax.random.fold_in(key, axis), (), 0, length) for axis, length in enumerate(entries.shape)]
    widest = entries.shape.index(max(entries.shape))
    next_to = index_at[:widest] + [(index_at[widest] + 1) % entries.shape[widest]] + index_at[widest + 1:]
    return entries.at[tuple(index_at)].set(least).at[tuple(next_to)].set(top_value)


def levels(key, dims, pieces, smallest, top_value):
    def one(axis_at, blocks):
        heights = jax.random.uniform(jax.random.fold_in(jax.random.fold_in(key, 6), axis_at), (blocks,), jnp.float32, smallest / len(pieces), top_value / len(pieces))
        return jnp.repeat(jnp.exp(heights), dims[axis_at] // blocks).reshape((-1,) + (1,) * (len(dims) - axis_at - 1))

    level = one(*pieces[0])
    for cut in pieces[1:]:
        level = level * one(*cut)
    return level


def scatter_about(stream_key, extent, deviation, bound, shards=(), held_as=jnp.bfloat16):
    drawn = deviation * jax.random.normal(stream_key, extent, jnp.float32)
    if shards:
        drawn = drawn * levels(stream_key, extent, shards, -0.22, 0.18)
    return jnp.clip(drawn, -bound, bound).astype(held_as)


def setup_inputs(seed: int = 0, part: int = 0) -> dict:
    seeds = jax.random.split(jax.random.key(seed), 12)
    own_keys = jax.random.split(jax.random.fold_in(seeds[11], part), 12)
    vel_index = place_ends(jax.random.randint(seeds[0], (NZ, NY, NX), 0, LEVELS), jax.random.fold_in(seeds[0], 1), 0, LEVELS - 1).astype(jnp.int32)
    courant = jnp.clip(jax.random.uniform(seeds[1], (LEVELS,), jnp.float32, 0.05, 0.19), 0.05, 0.19)
    src_now = scatter_about(own_keys[2], (NZ, NY, NX), 0.5, 4.0, ((0, 4), (1, 4)), jnp.float32)
    src_prev = scatter_about(own_keys[3], (NZ, NY, NX), 0.5, 4.0, ((0, 4), (1, 4)), jnp.float32)
    rec_now = scatter_about(own_keys[4], (NZ, NY, NX), 0.5, 4.0, ((0, 4), (1, 4)), jnp.float32)
    rec_prev = scatter_about(own_keys[5], (NZ, NY, NX), 0.5, 4.0, ((0, 4), (1, 4)), jnp.float32)
    src_pos = draw_src_pos(jax.random.fold_in(jax.random.fold_in(seeds[11], part), 71), part)
    src_wavelet = scatter_about(own_keys[7], (NSRC, STEPS), 4.0, 16.0, (), jnp.float32)
    rec_pos = draw_rec_pos(jax.random.fold_in(jax.random.fold_in(seeds[11], part), 71), part)
    rec_traces = scatter_about(own_keys[9], (NREC, STEPS), 4.0, 16.0, (), jnp.float32)
    offset_lags = draw_offset_lags(jax.random.fold_in(seeds[11], 71), part)
    return dict(vel_index=vel_index, courant=courant, src_now=src_now, src_prev=src_prev, rec_now=rec_now, rec_prev=rec_prev, src_pos=src_pos, src_wavelet=src_wavelet, rec_pos=rec_pos, rec_traces=rec_traces, offset_lags=offset_lags)


STENCIL_WEIGHTS = (-205.0 / 72.0, 8.0 / 5.0, -1.0 / 5.0, 8.0 / 315.0, -1.0 / 560.0)


def laplace(field):
    depth_cells, row_cells, col_cells = field.shape
    padded = jnp.pad(field, 4)

    def window(along_z, along_y, along_x):
        return padded[4 + along_z:4 + along_z + depth_cells, 4 + along_y:4 + along_y + row_cells, 4 + along_x:4 + along_x + col_cells]

    summed = (3.0 * STENCIL_WEIGHTS[0]) * field
    for distance in range(1, 5):
        weight = STENCIL_WEIGHTS[distance]
        pairs = window(distance, 0, 0) + window(-distance, 0, 0)
        pairs = pairs + window(0, distance, 0) + window(0, -distance, 0)
        pairs = pairs + window(0, 0, distance) + window(0, 0, -distance)
        summed = summed + weight * pairs
    return summed


def inject(shape, depth_at, row_at, col_at, amounts):
    return jnp.zeros(shape, jnp.float32).at[depth_at, row_at, col_at].add(amounts)


def reference(vel_index, courant, src_now, src_prev, rec_now, rec_prev, src_pos, src_wavelet, rec_pos, rec_traces, offset_lags):
    speed = courant[vel_index]
    shape = src_now.shape
    source, source_old = src_now, src_prev
    receiver, receiver_old = rec_now, rec_prev
    max_lag = NLAG // 2
    image_sum = jnp.zeros((NLAG,) + shape, jnp.float32)
    rec_depth = jnp.zeros_like(rec_pos[:, 0])
    for snapshot in range(IMAGES):
        for substep in range(SUB):
            tick_at = snapshot * SUB + substep
            source_term = inject(shape, src_pos[:, 0], src_pos[:, 1], src_pos[:, 2], src_wavelet[:, tick_at])
            receiver_term = inject(shape, rec_depth, rec_pos[:, 0], rec_pos[:, 1], rec_traces[:, tick_at])
            source_new = 2.0 * source - source_old + speed * (laplace(source) + source_term)
            receiver_new = 2.0 * receiver - receiver_old + speed * (laplace(receiver) + receiver_term)
            source_old, source = source, source_new
            receiver_old, receiver = receiver, receiver_new
        source_pad = jnp.pad(source, ((0, 0), (0, 0), (max_lag, max_lag)))
        receiver_pad = jnp.pad(receiver, ((0, 0), (0, 0), (max_lag, max_lag)))

        def add_lag(lag_slot, summed):
            lag_value = offset_lags[lag_slot]
            src_part = lax.dynamic_slice_in_dim(source_pad, (max_lag - lag_value).astype(jnp.int32), NX, 2)
            rec_part = lax.dynamic_slice_in_dim(receiver_pad, (max_lag + lag_value).astype(jnp.int32), NX, 2)
            return summed.at[lag_slot].add(src_part * rec_part)

        image_sum = lax.fori_loop(0, NLAG, add_lag, image_sum)
    padded = jnp.pad(image_sum, ((0, 0), (1, 1), (0, 0), (0, 0)))
    depth_cells = shape[0]
    filtered = 2.0 * padded[:, 1:1 + depth_cells] - padded[:, 0:depth_cells] - padded[:, 2:2 + depth_cells]
    return filtered.astype(jnp.bfloat16), source, receiver
```

```python
import functools

import jax
import jax.numpy as jnp
from jax import lax
from jax.experimental import pallas as pl
from jax.experimental.pallas import tpu as pltpu
from jax.sharding import PartitionSpec as P

SUB = 4
IMAGES = 4
HALO = 4
WINDOW_CELLS = 1 << 17
MESH = pl.DeviceIdType.MESH
WIRE = jnp.bfloat16


STENCIL_WEIGHTS = (-205.0 / 72.0, 8.0 / 5.0, -1.0 / 5.0, 8.0 / 315.0, -1.0 / 560.0)


def padded_2(block, sides, width):
    for axis, dim in sides:
        count = lax.axis_size(axis)
        forward = [(i, i + 1) for i in range(count - 1)]
        backward = [(target, source) for source, target in forward]
        low = lax.ppermute(
            lax.slice_in_dim(block, block.shape[dim] - width, None, axis=dim), axis, forward
        )
        high = lax.ppermute(lax.slice_in_dim(block, 0, width, axis=dim), axis, backward)
        block = jnp.concatenate([low, block, high], axis=dim)
    return block


def laplace(padded, depth_cells, row_cells, col_cells):

    def window(along_z, along_y, along_x):
        return padded[
            :,
            4 + along_z : 4 + along_z + depth_cells,
            4 + along_y : 4 + along_y + row_cells,
            4 + along_x : 4 + along_x + col_cells,
        ]

    summed = 3.0 * STENCIL_WEIGHTS[0] * window(0, 0, 0)
    for distance in range(1, 5):
        weight = STENCIL_WEIGHTS[distance]
        pairs = window(distance, 0, 0) + window(-distance, 0, 0)
        pairs = pairs + window(0, distance, 0) + window(0, -distance, 0)
        pairs = pairs + window(0, 0, distance) + window(0, 0, -distance)
        summed = summed + weight * pairs
    return summed


def lookup(vel_index, courant):
    levels = courant.shape[0]

    def add_level(level, summed):
        return summed + jnp.where(vel_index == level, courant[level], 0.0)

    return lax.fori_loop(0, levels, add_level, jnp.zeros(vel_index.shape, jnp.float32))


def local_index(global_at, start, extent):
    local_at = global_at - start
    inside = (local_at >= 0) & (local_at < extent)
    return jnp.where(inside, local_at, extent)


def inject_all(shape, depth_at, row_at, col_at, amounts):
    step_count = amounts.shape[1]
    return (
        jnp.zeros((step_count,) + shape, jnp.float32)
        .at[:, depth_at, row_at, col_at]
        .add(amounts.T, mode="drop")
    )


def lag_products(source_pad, receiver_pad, offset_lags, max_lag, col_cells):

    def product(lag_value):
        src_part = lax.dynamic_slice_in_dim(source_pad, max_lag - lag_value, col_cells, 2)
        rec_part = lax.dynamic_slice_in_dim(receiver_pad, max_lag + lag_value, col_cells, 2)
        return src_part * rec_part

    return jax.vmap(product)(offset_lags)


def depth_filter(padded, depth_cells):
    return (
        2.0 * padded[:, 1 : 1 + depth_cells]
        - padded[:, 0:depth_cells]
        - padded[:, 2 : 2 + depth_cells]
    )


def pad_inline(state, max_lag):
    return jnp.pad(state, ((0, 0), (0, 0), (0, 0), (max_lag, max_lag)))


def accumulate(slab_state, image_sum, edge_sum, offset_lags, max_lag):
    col_cells = slab_state.shape[3]
    padded = pad_inline(slab_state, max_lag)
    image_sum = image_sum + lag_products(padded[0], padded[1], offset_lags, max_lag, col_cells)
    return (image_sum, edge_sum)


def finish(image_sum):
    padded = padded_2(image_sum, (("role", 1),), 1)
    return depth_filter(padded, image_sum.shape[1]).astype(jnp.bfloat16)


def tile_shards(
    vel_index,
    courant,
    src_now,
    src_prev,
    rec_now,
    rec_prev,
    src_pos,
    src_wavelet,
    rec_pos,
    rec_traces,
    offset_lags,
):
    lag_count = offset_lags.shape[0]
    max_lag = lag_count // 2
    speed = lookup(vel_index, courant)
    band_start = lax.axis_index("band") * src_now.shape[1]
    role_at = lax.axis_index("role")
    current = jnp.stack([src_now, rec_now])
    previous = jnp.stack([src_prev, rec_prev])
    depth_start = role_at * src_now.shape[0]
    col_start = 0

    def faces(state):
        padded = padded_2(state, (("band", 2), ("role", 1)), 4)
        return jnp.pad(padded, ((0, 0), (0, 0), (0, 0), (4, 4)))

    depth_cells, row_cells, col_cells = speed.shape
    shape = speed.shape
    slab_shape = src_now.shape
    src_depth = local_index(src_pos[:, 0], depth_start, depth_cells)
    src_row = local_index(src_pos[:, 1], band_start, row_cells)
    src_col = local_index(src_pos[:, 2], col_start, col_cells)
    rec_depth = local_index(jnp.zeros_like(rec_pos[:, 0]), depth_start, depth_cells)
    rec_row = local_index(rec_pos[:, 0], band_start, row_cells)
    rec_col = local_index(rec_pos[:, 1], col_start, col_cells)
    src_terms = inject_all(shape, src_depth, src_row, src_col, src_wavelet)
    rec_terms = inject_all(shape, rec_depth, rec_row, rec_col, rec_traces)
    image_sum = jnp.zeros((lag_count,) + slab_shape, jnp.float32)
    edge_sum = jnp.zeros((lag_count, 2) + slab_shape[1:], jnp.float32)
    slab_state = current
    for snapshot in range(IMAGES):

        def advance(substep, carry):
            state, older = carry
            tick_at = snapshot * SUB + substep
            sources = jnp.stack(
                [
                    lax.dynamic_index_in_dim(src_terms, tick_at, 0, keepdims=False),
                    lax.dynamic_index_in_dim(rec_terms, tick_at, 0, keepdims=False),
                ]
            )
            laplacian = laplace(faces(state), depth_cells, row_cells, col_cells)
            updated = 2.0 * state - older + speed * (laplacian + sources)
            return (updated, state)

        current, previous = lax.fori_loop(0, SUB, advance, (current, previous))
        slab_state = current
        image_sum, edge_sum = accumulate(slab_state, image_sum, edge_sum, offset_lags, max_lag)
    image = finish(image_sum)
    return (image, slab_state[0], slab_state[1])


def split_two(value):
    high = value.astype(jnp.bfloat16)
    low = (value - high.astype(jnp.float32)).astype(jnp.bfloat16)
    return high, low


def inline_matrix(cols):
    row = lax.broadcasted_iota(jnp.int32, (cols, cols), 0)
    col = lax.broadcasted_iota(jnp.int32, (cols, cols), 1)
    apart = jnp.abs(row - col)
    matrix = jnp.where(apart == 0, 3.0 * STENCIL_WEIGHTS[0], 0.0)
    for distance in range(1, 5):
        matrix = jnp.where(apart == distance, STENCIL_WEIGHTS[distance], matrix)
    return matrix


def window_kernel(
    bands,
    roles,
    vel_ref,
    courant_ref,
    src_now_ref,
    src_prev_ref,
    rec_now_ref,
    rec_prev_ref,
    src_pos_ref,
    src_wave_ref,
    rec_pos_ref,
    rec_trace_ref,
    lags_ref,
    image_ref,
    src_out_ref,
    rec_out_ref,
    out_buf,
    blocks,
    field_a,
    field_b,
    speed_ref,
    split_ref,
    inline_ref,
    base_ref,
    inject_ref,
    stage_ref,
    snap_ref,
    near_send,
    far_send,
    block_recv,
    snap_send,
    snap_recv,
):
    depth, rows, cols = vel_ref.shape
    full_z, full_y = depth * roles, rows * bands
    cells = depth * rows
    columns = roles // 2
    survey = lax.axis_index("survey")
    band = lax.axis_index("band")
    role = lax.axis_index("role")
    core = lax.rem(role, 2)
    column = role // 2
    own = band * roles + role
    f32 = jnp.float32
    y0 = 8

    def device(at_band, at_role):
        return (survey, at_band, at_role)

    partner = device(band, 2 * column + 1 - core)
    barrier = pltpu.get_barrier_semaphore()
    greeted = 0
    for step in range(1, bands):
        for side in range(2):
            pl.semaphore_signal(
                barrier,
                inc=1,
                device_id=device(lax.rem(band + step, bands), 2 * column + side),
                device_id_type=MESH,
            )
            greeted += 1
    pl.semaphore_signal(barrier, inc=1, device_id=partner, device_id_type=MESH)
    greeted += 1
    for step in range(1, columns):
        pl.semaphore_signal(
            barrier,
            inc=1,
            device_id=device(band, 2 * lax.rem(column + step, columns) + core),
            device_id_type=MESH,
        )
        greeted += 1

    index = vel_ref[...].astype(f32).reshape(cells, cols)
    for side, now_ref, prev_ref in ((0, src_now_ref, src_prev_ref), (1, rec_now_ref, rec_prev_ref)):
        now = now_ref[...].reshape(cells, cols)
        change = now - prev_ref[...].reshape(cells, cols)
        out_buf[side, 0:cells] = now.astype(WIRE)
        out_buf[side, cells : 2 * cells] = change.astype(WIRE)
        out_buf[side, 2 * cells : 3 * cells] = index.astype(WIRE)
    pl.semaphore_wait(barrier, greeted)

    sends = []
    for step in range(1, bands):
        for side in range(2):
            copy = pltpu.make_async_remote_copy(
                src_ref=out_buf.at[side],
                dst_ref=blocks.at[own],
                send_sem=near_send.at[2 * step + side],
                recv_sem=block_recv.at[own],
                device_id=device(lax.rem(band + step, bands), 2 * column + side),
                device_id_type=MESH,
            )
            copy.start()
            sends.append(copy)
    copy = pltpu.make_async_remote_copy(
        src_ref=out_buf.at[1 - core],
        dst_ref=blocks.at[own],
        send_sem=near_send.at[0],
        recv_sem=block_recv.at[own],
        device_id=partner,
        device_id_type=MESH,
    )
    copy.start()
    sends.append(copy)

    def pass_on(step, source, slot, lane):
        copy = pltpu.make_async_remote_copy(
            src_ref=source,
            dst_ref=blocks.at[slot],
            send_sem=far_send.at[lane],
            recv_sem=block_recv.at[slot],
            device_id=device(band, 2 * lax.rem(column + step, columns) + core),
            device_id_type=MESH,
        )
        copy.start()
        sends.append(copy)

    def landed(slot):
        pltpu.make_async_copy(blocks.at[slot], blocks.at[slot], block_recv.at[slot]).wait()

    for step in range(1, columns):
        pass_on(step, out_buf.at[core], own, step)

    inject_ref[...] = jnp.zeros_like(inject_ref)
    lines = split_ref.shape[0]
    half = cols // 2
    row_at = lax.broadcasted_iota(jnp.int32, (lines, cols), 0)
    lane_at = lax.broadcasted_iota(jnp.int32, (lines, cols), 1)
    lane_low = jnp.where(lane_at >= half, lane_at - half, lane_at)
    steps = inject_ref.shape[0]

    @pl.when(core == 0)
    def _():
        count = src_pos_ref.shape[0]
        target = jnp.full((1, cols), -1, jnp.int32)
        lane = lax.broadcasted_iota(jnp.int32, (1, cols), 1)
        lane = jnp.where(lane >= half, lane - half, lane)
        for source in range(count):
            line = src_pos_ref[source, 0] * full_y + src_pos_ref[source, 1]
            target = jnp.where(lane == source, line, target)
        split_ref[:, 2 * cols : 3 * cols] = jnp.where(row_at == target, 1.0, 0.0).astype(jnp.bfloat16)
        height = -(-count // 16) * 16
        row = lax.broadcasted_iota(jnp.int32, (height, cols), 0)
        col = lax.broadcasted_iota(jnp.int32, (height, cols), 1)
        for tick in range(steps):
            term = jnp.zeros((height, cols), f32)
            for source in range(count):
                here = (row == source) & (col == src_pos_ref[source, 2])
                term = jnp.where(here, src_wave_ref[source, tick], term)
            high, low = split_two(term)
            inject_ref[tick, 0:height] = high
            inject_ref[tick, half : half + height] = low

    @pl.when(core == 1)
    def _():
        split_ref[:, 2 * cols : 3 * cols] = jnp.where(
            (row_at < full_y) & (row_at == lane_low), 1.0, 0.0
        ).astype(jnp.bfloat16)
        count = rec_pos_ref.shape[1]
        chunk = min(512, count)
        total = jnp.zeros((2 * steps * full_y, cols), f32)
        for at in range(0, count, chunk):
            size = min(chunk, count - at)
            y_at = rec_pos_ref[0:1, at : at + size]
            x_at = rec_pos_ref[1:2, at : at + size]
            in_row = lax.broadcasted_iota(jnp.int32, (full_y, size), 0) == y_at
            in_col = lax.broadcasted_iota(jnp.int32, (cols, size), 0) == x_at
            in_col = jnp.where(in_col, 1.0, 0.0).astype(jnp.bfloat16)
            amounts = rec_trace_ref[:, at : at + size]
            high = amounts.astype(jnp.bfloat16).astype(f32)
            parts = []
            for part in (high, amounts - high):
                for tick in range(steps):
                    parts.append(jnp.where(in_row, part[tick : tick + 1], 0.0).astype(jnp.bfloat16))
            total = total + lax.dot_general(
                jnp.concatenate(parts, axis=0),
                in_col,
                (((1,), (1,)), ((), ())),
                preferred_element_type=f32,
            )
        size = steps * full_y
        high, low = split_two(total[0:size] + total[size : 2 * size])
        for tick in range(steps):
            inject_ref[tick, 0:full_y] = high[tick * full_y : (tick + 1) * full_y]
            inject_ref[tick, half : half + full_y] = low[tick * full_y : (tick + 1) * full_y]

    high, low = split_two(inline_matrix(cols))
    base_ref[0:cols] = high
    base_ref[cols : 2 * cols] = high
    base_ref[2 * cols : 3 * cols] = low
    field_a[...] = jnp.zeros_like(field_a)
    field_b[...] = jnp.zeros_like(field_b)

    slot = band * roles + 2 * column + 1 - core
    landed(slot)
    for step in range(1, columns):
        pass_on(step, blocks.at[slot], slot, columns + step)
    for hop in range(1, bands):
        for side in range(2):
            slot = lax.rem(band + hop, bands) * roles + 2 * column + side
            landed(slot)
            for step in range(1, columns):
                pass_on(step, blocks.at[slot], slot, (2 * hop + side) * columns + step)
    for step in range(1, columns):
        other = lax.rem(column + step, columns)
        for at_band in range(bands):
            for side in range(2):
                landed(at_band * roles + 2 * other + side)
    blocks[own] = out_buf[core]

    def table(values):
        found = jnp.zeros(values.shape, f32)
        for level in range(courant_ref.shape[0]):
            found = jnp.where(values == float(level), courant_ref[level], found)
        return found

    for at_role in range(roles):
        for at_band in range(bands):
            block = blocks[at_band * roles + at_role].astype(f32)
            now = block[0:cells].reshape(depth, rows, cols)
            prev = now - block[cells : 2 * cells].reshape(depth, rows, cols)
            z_part = pl.ds(HALO + depth * at_role, depth)
            y_part = pl.ds(y0 + rows * at_band, rows)
            field_a[z_part, y_part, :] = now
            field_b[z_part, y_part, :] = prev
            speed_ref[pl.ds(depth * at_role, depth), pl.ds(rows * at_band, rows), :] = table(
                block[2 * cells : 3 * cells]
            ).reshape(depth, rows, cols)

    own_z = pl.ds(HALO + depth * role, depth)
    own_y = pl.ds(pl.multiple_of(y0 + rows * band, rows), rows)
    field_a[own_z, own_y, :] = jnp.where(core == 0, src_now_ref[...], rec_now_ref[...])
    field_b[own_z, own_y, :] = jnp.where(core == 0, src_prev_ref[...], rec_prev_ref[...])

    def store_split(z_at, value):
        high, low = split_two(value)
        split_ref[pl.ds(z_at * full_y, full_y), 0:cols] = low
        split_ref[pl.ds(z_at * full_y, full_y), cols : 2 * cols] = high

    for z_at in range(full_z):
        store_split(z_at, field_a[HALO + z_at, y0 : y0 + full_y, :])

    def advance(tick, state, older):
        weights = jnp.concatenate([base_ref[2 * cols : 3 * cols], inject_ref[tick]], axis=0)
        inline_ref[...] = jnp.dot(
            split_ref[:, 0 : 2 * cols], base_ref[0 : 2 * cols], preferred_element_type=f32
        ) + jnp.dot(split_ref[:, cols : 3 * cols], weights, preferred_element_type=f32)
        for z_at in range(full_z):
            total = inline_ref[z_at * full_y : (z_at + 1) * full_y]
            z_in = HALO + z_at
            centre = state[z_in, y0 : y0 + full_y, :]
            for distance in range(1, 5):
                pairs = state[z_in - distance, y0 : y0 + full_y, :] + state[z_in + distance, y0 : y0 + full_y, :]
                pairs = pairs + (
                    state[z_in, y0 - distance : y0 - distance + full_y, :]
                    + state[z_in, y0 + distance : y0 + distance + full_y, :]
                )
                total = total + STENCIL_WEIGHTS[distance] * pairs
            updated = (2.0 * centre - older[z_in, y0 : y0 + full_y, :]) + speed_ref[z_at] * total
            older[z_in, y0 : y0 + full_y, :] = updated
            store_split(z_at, updated)

    partner_role = 2 * column + 1 - core
    deep = depth + 2

    def snap_copy(snapshot):
        return pltpu.make_async_remote_copy(
            src_ref=stage_ref.at[snapshot],
            dst_ref=snap_ref.at[snapshot, core],
            send_sem=snap_send.at[snapshot],
            recv_sem=snap_recv.at[snapshot],
            device_id=partner,
            device_id_type=MESH,
        )

    def one_image(snapshot, carry):
        for pair in range(SUB // 2):
            advance(SUB * snapshot + 2 * pair, field_a, field_b)
            advance(SUB * snapshot + 2 * pair + 1, field_b, field_a)
        stage_ref[snapshot] = field_a[pl.ds(HALO - 1 + depth * partner_role, deep), own_y, :]
        snap_copy(snapshot).start()
        snap_ref[snapshot, core] = field_a[pl.ds(HALO - 1 + depth * role, deep), own_y, :]
        return carry

    lax.fori_loop(0, IMAGES, one_image, 0)
    for snapshot in range(IMAGES):
        snap_copy(snapshot).wait()
    src_out_ref[...] = snap_ref[IMAGES - 1, 0, 1 : 1 + depth]
    rec_out_ref[...] = snap_ref[IMAGES - 1, 1, 1 : 1 + depth]

    def one_lag(slot, carry):
        lag = lags_ref[slot]
        back = jnp.where(lag > 0, cols - 2 * lag, -2 * lag)
        shift = jnp.where(lag < 0, cols + lag, lag)
        summed = jnp.zeros((deep * rows, cols), f32)
        for snapshot in range(IMAGES):
            moved = pltpu.roll(snap_ref[snapshot, 1].reshape(deep * rows, cols), back, 1)
            summed = summed + snap_ref[snapshot, 0].reshape(deep * rows, cols) * moved
        filtered = (
            2.0 * summed[rows : rows + cells] - summed[0:cells] - summed[2 * rows : 2 * rows + cells]
        )
        filtered = pltpu.roll(filtered, shift, 1)
        lane = lax.broadcasted_iota(jnp.int32, (cells, cols), 1)
        reach = jnp.abs(lag)
        inside = (lane >= reach) & (lane < cols - reach)
        image_ref[slot] = jnp.where(inside, filtered, 0.0).reshape(depth, rows, cols)
        return carry

    lax.fori_loop(0, lags_ref.shape[0], one_lag, 0, unroll=2)
    for copy in sends:
        copy.wait_send()


def window_shards(bands, roles, *arrays):
    (vel_index, courant, src_now, src_prev, rec_now, rec_prev) = arrays[:6]
    (src_pos, src_wavelet, rec_pos, rec_traces, offset_lags) = arrays[6:]
    depth, rows, cols = vel_index.shape
    cells = depth * rows
    full_z, full_y = depth * roles, rows * bands
    lag_count = offset_lags.shape[0]
    columns = roles // 2
    steps = SUB * IMAGES
    f32, bf16 = jnp.float32, jnp.bfloat16
    vmem = pl.BlockSpec(memory_space=pltpu.VMEM)
    smem = pl.BlockSpec(memory_space=pltpu.SMEM)
    padded = (full_z + 2 * HALO, full_y + 16, cols)
    image, source, receiver = pl.pallas_call(
        functools.partial(window_kernel, bands, roles),
        out_shape=(
            jax.ShapeDtypeStruct((lag_count, depth, rows, cols), f32),
            jax.ShapeDtypeStruct((depth, rows, cols), f32),
            jax.ShapeDtypeStruct((depth, rows, cols), f32),
        ),
        in_specs=[vmem, smem, vmem, vmem, vmem, vmem, smem, smem, vmem, vmem, smem],
        out_specs=(vmem, vmem, vmem),
        scratch_shapes=[
            pltpu.VMEM((2, 3 * cells, cols), WIRE),
            pltpu.VMEM((bands * roles, 3 * cells, cols), WIRE),
            pltpu.VMEM(padded, f32),
            pltpu.VMEM(padded, f32),
            pltpu.VMEM((full_z, full_y, cols), f32),
            pltpu.VMEM((full_z * full_y, 3 * cols), bf16),
            pltpu.VMEM((full_z * full_y, cols), f32),
            pltpu.VMEM((3 * cols, cols), bf16),
            pltpu.VMEM((steps, cols, cols), bf16),
            pltpu.VMEM((IMAGES, depth + 2, rows, cols), f32),
            pltpu.VMEM((IMAGES, 2, depth + 2, rows, cols), f32),
            pltpu.SemaphoreType.DMA((2 * bands,)),
            pltpu.SemaphoreType.DMA((2 * bands * columns,)),
            pltpu.SemaphoreType.DMA((bands * roles,)),
            pltpu.SemaphoreType.DMA((IMAGES,)),
            pltpu.SemaphoreType.DMA((IMAGES,)),
        ],
        compiler_params=pltpu.CompilerParams(
            collective_id=0, has_side_effects=True, vmem_limit_bytes=48 * 1024 * 1024
        ),
    )(
        vel_index,
        courant,
        src_now,
        src_prev,
        rec_now,
        rec_prev,
        src_pos,
        src_wavelet,
        rec_pos.T,
        rec_traces.T,
        offset_lags,
    )
    return image.astype(bf16), source, receiver


def shards(bands, roles, *arrays):
    depth, rows, cols = arrays[0].shape
    sources = arrays[6].shape[0]
    small = depth * roles * rows * bands * cols <= WINDOW_CELLS
    fits = roles % 2 == 0 and rows % 8 == 0 and cols % 128 == 0
    fits = fits and max(rows * bands, sources) <= cols // 2 and arrays[10].shape[0] < cols
    fits = fits and (depth * rows) % 16 == 0 and arrays[1].shape[0] <= 256
    if small and fits:
        return window_shards(bands, roles, *arrays)
    return tile_shards(*arrays)


def solution(mesh):
    placed = (
        P("role", "band", None),
        P(),
        P(("survey", "role"), "band", None),
        P(("survey", "role"), "band", None),
        P(("survey", "role"), "band", None),
        P(("survey", "role"), "band", None),
        P("survey", None),
        P("survey", None),
        P("survey", None),
        P("survey", None),
        P(),
    )
    return jax.shard_map(
        functools.partial(shards, mesh.shape["band"], mesh.shape["role"]),
        mesh=mesh,
        in_specs=placed,
        out_specs=(
            P("survey", "role", "band", None),
            P(("survey", "role"), "band", None),
            P(("survey", "role"), "band", None),
        ),
        check_vma=False,
    )
```

```python
import functools

import jax
import jax.numpy as jnp
from jax import lax
from jax.experimental import pallas as pl
from jax.experimental.pallas import tpu as pltpu
from jax.sharding import PartitionSpec as P

SUB = 4
IMAGES = 4
HALO = 4
WINDOW_CELLS = 1 << 17
MESH = pl.DeviceIdType.MESH
WIRE = jnp.bfloat16


STENCIL_WEIGHTS = (-205.0 / 72.0, 8.0 / 5.0, -1.0 / 5.0, 8.0 / 315.0, -1.0 / 560.0)


def padded_2(block, sides, width):
    for axis, dim in sides:
        count = lax.axis_size(axis)
        forward = [(i, i + 1) for i in range(count - 1)]
        backward = [(target, source) for source, target in forward]
        low = lax.ppermute(
            lax.slice_in_dim(block, block.shape[dim] - width, None, axis=dim), axis, forward
        )
        high = lax.ppermute(lax.slice_in_dim(block, 0, width, axis=dim), axis, backward)
        block = jnp.concatenate([low, block, high], axis=dim)
    return block


def laplace(padded, depth_cells, row_cells, col_cells):

    def window(along_z, along_y, along_x):
        return padded[
            :,
            4 + along_z : 4 + along_z + depth_cells,
            4 + along_y : 4 + along_y + row_cells,
            4 + along_x : 4 + along_x + col_cells,
        ]

    summed = 3.0 * STENCIL_WEIGHTS[0] * window(0, 0, 0)
    for distance in range(1, 5):
        weight = STENCIL_WEIGHTS[distance]
        pairs = window(distance, 0, 0) + window(-distance, 0, 0)
        pairs = pairs + window(0, distance, 0) + window(0, -distance, 0)
        pairs = pairs + window(0, 0, distance) + window(0, 0, -distance)
        summed = summed + weight * pairs
    return summed


def lookup(vel_index, courant):
    levels = courant.shape[0]

    def add_level(level, summed):
        return summed + jnp.where(vel_index == level, courant[level], 0.0)

    return lax.fori_loop(0, levels, add_level, jnp.zeros(vel_index.shape, jnp.float32))


def local_index(global_at, start, extent):
    local_at = global_at - start
    inside = (local_at >= 0) & (local_at < extent)
    return jnp.where(inside, local_at, extent)


def inject_all(shape, depth_at, row_at, col_at, amounts):
    step_count = amounts.shape[1]
    return (
        jnp.zeros((step_count,) + shape, jnp.float32)
        .at[:, depth_at, row_at, col_at]
        .add(amounts.T, mode="drop")
    )


def lag_products(source_pad, receiver_pad, offset_lags, max_lag, col_cells):

    def product(lag_value):
        src_part = lax.dynamic_slice_in_dim(source_pad, max_lag - lag_value, col_cells, 2)
        rec_part = lax.dynamic_slice_in_dim(receiver_pad, max_lag + lag_value, col_cells, 2)
        return src_part * rec_part

    return jax.vmap(product)(offset_lags)


def depth_filter(padded, depth_cells):
    return (
        2.0 * padded[:, 1 : 1 + depth_cells]
        - padded[:, 0:depth_cells]
        - padded[:, 2 : 2 + depth_cells]
    )


def pad_inline(state, max_lag):
    return jnp.pad(state, ((0, 0), (0, 0), (0, 0), (max_lag, max_lag)))


def accumulate(slab_state, image_sum, edge_sum, offset_lags, max_lag):
    col_cells = slab_state.shape[3]
    padded = pad_inline(slab_state, max_lag)
    image_sum = image_sum + lag_products(padded[0], padded[1], offset_lags, max_lag, col_cells)
    return (image_sum, edge_sum)


def finish(image_sum):
    padded = padded_2(image_sum, (("role", 1),), 1)
    return depth_filter(padded, image_sum.shape[1]).astype(jnp.bfloat16)


def tile_shards(
    vel_index,
    courant,
    src_now,
    src_prev,
    rec_now,
    rec_prev,
    src_pos,
    src_wavelet,
    rec_pos,
    rec_traces,
    offset_lags,
):
    lag_count = offset_lags.shape[0]
    max_lag = lag_count // 2
    speed = lookup(vel_index, courant)
    band_start = lax.axis_index("band") * src_now.shape[1]
    role_at = lax.axis_index("role")
    current = jnp.stack([src_now, rec_now])
    previous = jnp.stack([src_prev, rec_prev])
    depth_start = role_at * src_now.shape[0]
    col_start = 0

    def faces(state):
        padded = padded_2(state, (("band", 2), ("role", 1)), 4)
        return jnp.pad(padded, ((0, 0), (0, 0), (0, 0), (4, 4)))

    depth_cells, row_cells, col_cells = speed.shape
    shape = speed.shape
    slab_shape = src_now.shape
    src_depth = local_index(src_pos[:, 0], depth_start, depth_cells)
    src_row = local_index(src_pos[:, 1], band_start, row_cells)
    src_col = local_index(src_pos[:, 2], col_start, col_cells)
    rec_depth = local_index(jnp.zeros_like(rec_pos[:, 0]), depth_start, depth_cells)
    rec_row = local_index(rec_pos[:, 0], band_start, row_cells)
    rec_col = local_index(rec_pos[:, 1], col_start, col_cells)
    src_terms = inject_all(shape, src_depth, src_row, src_col, src_wavelet)
    rec_terms = inject_all(shape, rec_depth, rec_row, rec_col, rec_traces)
    image_sum = jnp.zeros((lag_count,) + slab_shape, jnp.float32)
    edge_sum = jnp.zeros((lag_count, 2) + slab_shape[1:], jnp.float32)
    slab_state = current
    for snapshot in range(IMAGES):

        def advance(substep, carry):
            state, older = carry
            tick_at = snapshot * SUB + substep
            sources = jnp.stack(
                [
                    lax.dynamic_index_in_dim(src_terms, tick_at, 0, keepdims=False),
                    lax.dynamic_index_in_dim(rec_terms, tick_at, 0, keepdims=False),
                ]
            )
            laplacian = laplace(faces(state), depth_cells, row_cells, col_cells)
            updated = 2.0 * state - older + speed * (laplacian + sources)
            return (updated, state)

        current, previous = lax.fori_loop(0, SUB, advance, (current, previous))
        slab_state = current
        image_sum, edge_sum = accumulate(slab_state, image_sum, edge_sum, offset_lags, max_lag)
    image = finish(image_sum)
    return (image, slab_state[0], slab_state[1])


def split_two(value):
    high = value.astype(jnp.bfloat16)
    low = (value - high.astype(jnp.float32)).astype(jnp.bfloat16)
    return high, low


def inline_matrix(cols):
    row = lax.broadcasted_iota(jnp.int32, (cols, cols), 0)
    col = lax.broadcasted_iota(jnp.int32, (cols, cols), 1)
    apart = jnp.abs(row - col)
    matrix = jnp.where(apart == 0, 3.0 * STENCIL_WEIGHTS[0], 0.0)
    for distance in range(1, 5):
        matrix = jnp.where(apart == distance, STENCIL_WEIGHTS[distance], matrix)
    return matrix


def window_kernel(
    bands,
    roles,
    *refs,
):
    inputs, outputs, held = refs[:11], refs[11:14], refs[14:25]
    (
        vel_ref,
        courant_ref,
        src_now_ref,
        src_prev_ref,
        rec_now_ref,
        rec_prev_ref,
        src_pos_ref,
        src_wave_ref,
        rec_pos_ref,
        rec_trace_ref,
        lags_ref,
    ) = held
    image_ref, src_out_ref, rec_out_ref = outputs
    (
        out_buf,
        blocks,
        field_a,
        field_b,
        speed_ref,
        split_ref,
        inline_ref,
        base_ref,
        inject_ref,
        stage_ref,
        snap_ref,
        near_send,
        far_send,
        block_recv,
        snap_send,
        snap_recv,
        lend_ref,
        in_sem,
        lend_send,
        lend_recv,
    ) = refs[25:]
    fetches = [
        pltpu.make_async_copy(given, kept, in_sem.at[at])
        for at, (given, kept) in enumerate(zip(inputs, held))
    ]
    for fetch in fetches:
        fetch.start()
    inject_ref[...] = jnp.zeros_like(inject_ref)
    depth, rows, cols = vel_ref.shape
    full_z, full_y = depth * roles, rows * bands
    cells = depth * rows
    columns = roles // 2
    survey = lax.axis_index("survey")
    band = lax.axis_index("band")
    role = lax.axis_index("role")
    core = lax.rem(role, 2)
    column = role // 2
    own = band * roles + role
    f32 = jnp.float32
    y0 = 8

    def device(at_band, at_role):
        return (survey, at_band, at_role)

    partner = device(band, 2 * column + 1 - core)
    barrier = pltpu.get_barrier_semaphore()
    greeted = 0
    for step in range(1, bands):
        for side in range(2):
            pl.semaphore_signal(
                barrier,
                inc=1,
                device_id=device(lax.rem(band + step, bands), 2 * column + side),
                device_id_type=MESH,
            )
            greeted += 1
    pl.semaphore_signal(barrier, inc=1, device_id=partner, device_id_type=MESH)
    greeted += 1
    for step in range(1, columns):
        pl.semaphore_signal(
            barrier,
            inc=1,
            device_id=device(band, 2 * lax.rem(column + step, columns) + core),
            device_id_type=MESH,
        )
        greeted += 1

    for at in (0, 2, 3, 4, 5):
        fetches[at].wait()
    index = vel_ref[...].astype(f32).reshape(cells, cols)
    for side, now_ref, prev_ref in ((0, src_now_ref, src_prev_ref), (1, rec_now_ref, rec_prev_ref)):
        now = now_ref[...].reshape(cells, cols)
        change = now - prev_ref[...].reshape(cells, cols)
        out_buf[side, 0:cells] = now.astype(WIRE)
        out_buf[side, cells : 2 * cells] = change.astype(WIRE)
        out_buf[side, 2 * cells : 3 * cells] = index.astype(WIRE)
    pl.semaphore_wait(barrier, greeted)

    sends = []
    for step in range(1, bands):
        for side in range(2):
            copy = pltpu.make_async_remote_copy(
                src_ref=out_buf.at[side],
                dst_ref=blocks.at[own],
                send_sem=near_send.at[2 * step + side],
                recv_sem=block_recv.at[own],
                device_id=device(lax.rem(band + step, bands), 2 * column + side),
                device_id_type=MESH,
            )
            copy.start()
            sends.append(copy)
    copy = pltpu.make_async_remote_copy(
        src_ref=out_buf.at[1 - core],
        dst_ref=blocks.at[own],
        send_sem=near_send.at[0],
        recv_sem=block_recv.at[own],
        device_id=partner,
        device_id_type=MESH,
    )
    copy.start()
    sends.append(copy)

    def pass_on(step, source, slot, lane):
        copy = pltpu.make_async_remote_copy(
            src_ref=source,
            dst_ref=blocks.at[slot],
            send_sem=far_send.at[lane],
            recv_sem=block_recv.at[slot],
            device_id=device(band, 2 * lax.rem(column + step, columns) + core),
            device_id_type=MESH,
        )
        copy.start()
        sends.append(copy)

    def landed(slot):
        pltpu.make_async_copy(blocks.at[slot], blocks.at[slot], block_recv.at[slot]).wait()

    for step in range(1, columns):
        pass_on(step, out_buf.at[core], own, step)

    for at in (1, 6, 7, 8, 9, 10):
        fetches[at].wait()
    lines = split_ref.shape[0]
    half = cols // 2
    row_at = lax.broadcasted_iota(jnp.int32, (lines, cols), 0)
    lane_at = lax.broadcasted_iota(jnp.int32, (lines, cols), 1)
    lane_low = jnp.where(lane_at >= half, lane_at - half, lane_at)
    steps = inject_ref.shape[0]

    @pl.when(core == 0)
    def _():
        count = src_pos_ref.shape[0]
        target = jnp.full((1, cols), -1, jnp.int32)
        lane = lax.broadcasted_iota(jnp.int32, (1, cols), 1)
        lane = jnp.where(lane >= half, lane - half, lane)
        for source in range(count):
            line = src_pos_ref[source, 0] * full_y + src_pos_ref[source, 1]
            target = jnp.where(lane == source, line, target)
        split_ref[:, 2 * cols : 3 * cols] = jnp.where(row_at == target, 1.0, 0.0).astype(jnp.bfloat16)
        height = -(-count // 16) * 16
        row = lax.broadcasted_iota(jnp.int32, (height, cols), 0)
        col = lax.broadcasted_iota(jnp.int32, (height, cols), 1)
        for tick in range(steps):
            term = jnp.zeros((height, cols), f32)
            for source in range(count):
                here = (row == source) & (col == src_pos_ref[source, 2])
                term = jnp.where(here, src_wave_ref[source, tick], term)
            high, low = split_two(term)
            inject_ref[tick, 0:height] = high
            inject_ref[tick, half : half + height] = low

    high, low = split_two(inline_matrix(cols))
    base_ref[0:cols] = high
    base_ref[cols : 2 * cols] = high
    base_ref[2 * cols : 3 * cols] = low
    field_a[...] = jnp.zeros_like(field_a)
    field_b[...] = jnp.zeros_like(field_b)

    @pl.when(core == 1)
    def _():
        split_ref[:, 2 * cols : 3 * cols] = jnp.where(
            (row_at < full_y) & (row_at == lane_low), 1.0, 0.0
        ).astype(jnp.bfloat16)

    share = steps // 2
    first = pl.multiple_of(share * (1 - core), share)
    count = rec_pos_ref.shape[1]
    chunk = min(512, count)

    def add_receivers(total, start, stop):
        for at in range(start, stop, chunk):
            size = min(chunk, stop - at)
            y_at = rec_pos_ref[0:1, at : at + size]
            x_at = rec_pos_ref[1:2, at : at + size]
            in_row = lax.broadcasted_iota(jnp.int32, (full_y, size), 0) == y_at
            in_col = lax.broadcasted_iota(jnp.int32, (cols, size), 0) == x_at
            in_col = jnp.where(in_col, 1.0, 0.0).astype(jnp.bfloat16)
            amounts = rec_trace_ref[pl.ds(first, share), at : at + size]
            high = amounts.astype(jnp.bfloat16).astype(f32)
            parts = []
            for part in (high, amounts - high):
                for tick in range(share):
                    parts.append(jnp.where(in_row, part[tick : tick + 1], 0.0).astype(jnp.bfloat16))
            total = total + lax.dot_general(
                jnp.concatenate(parts, axis=0),
                in_col,
                (((1,), (1,)), ((), ())),
                preferred_element_type=f32,
            )
        return total

    middle = count // 2 // chunk * chunk
    added = add_receivers(jnp.zeros((2 * share * full_y, cols), f32), 0, middle)

    slot = band * roles + 2 * column + 1 - core
    landed(slot)
    for step in range(1, columns):
        pass_on(step, blocks.at[slot], slot, columns + step)
    for hop in range(1, bands):
        for side in range(2):
            slot = lax.rem(band + hop, bands) * roles + 2 * column + side
            landed(slot)
            for step in range(1, columns):
                pass_on(step, blocks.at[slot], slot, (2 * hop + side) * columns + step)
    added = add_receivers(added, middle, count)
    size = share * full_y
    high, low = split_two(added[0:size] + added[size : 2 * size])
    lend_ref[0] = high.reshape(share, full_y, cols)
    lend_ref[1] = low.reshape(share, full_y, cols)

    def lend_copy(part):
        return pltpu.make_async_remote_copy(
            src_ref=lend_ref.at[part],
            dst_ref=inject_ref.at[pl.ds(share, share), pl.ds(part * half, full_y)],
            send_sem=lend_send.at[part],
            recv_sem=lend_recv.at[part],
            device_id=partner,
            device_id_type=MESH,
        )

    @pl.when(core == 0)
    def _():
        for part in range(2):
            lend_copy(part).start()

    @pl.when(core == 1)
    def _():
        for part in range(2):
            inject_ref[0:share, part * half : part * half + full_y] = lend_ref[part]

    def table(values):
        found = jnp.zeros(values.shape, f32)
        for level in range(courant_ref.shape[0]):
            found = jnp.where(values == float(level), courant_ref[level], found)
        return found

    def unpack(at_band, at_role, block):
        now = block[0:cells].reshape(depth, rows, cols)
        prev = now - block[cells : 2 * cells].reshape(depth, rows, cols)
        z_part = pl.ds(HALO + depth * at_role, depth)
        y_part = pl.ds(pl.multiple_of(y0 + rows * at_band, rows), rows)
        field_a[z_part, y_part, :] = now
        field_b[z_part, y_part, :] = prev
        speed_ref[pl.ds(depth * at_role, depth), pl.ds(pl.multiple_of(rows * at_band, rows), rows), :] = table(
            block[2 * cells : 3 * cells]
        ).reshape(depth, rows, cols)

    for hop in range(bands):
        for side in range(2):
            at_band, at_role = lax.rem(band + hop, bands), 2 * column + lax.rem(core + side, 2)
            if hop == 0 and side == 0:
                unpack(band, role, out_buf[core].astype(f32))
            else:
                unpack(at_band, at_role, blocks[at_band * roles + at_role].astype(f32))
    for hop in range(bands):
        for step in range(1, columns):
            for side in range(2):
                at_band = lax.rem(band + hop, bands)
                at_role = 2 * lax.rem(column + step, columns) + lax.rem(core + side, 2)
                landed(at_band * roles + at_role)
                unpack(at_band, at_role, blocks[at_band * roles + at_role].astype(f32))

    own_z = pl.ds(HALO + depth * role, depth)
    own_y = pl.ds(pl.multiple_of(y0 + rows * band, rows), rows)
    field_a[own_z, own_y, :] = jnp.where(core == 0, src_now_ref[...], rec_now_ref[...])
    field_b[own_z, own_y, :] = jnp.where(core == 0, src_prev_ref[...], rec_prev_ref[...])

    def store_split(z_at, value):
        high, low = split_two(value)
        split_ref[pl.ds(z_at * full_y, full_y), 0:cols] = low
        split_ref[pl.ds(z_at * full_y, full_y), cols : 2 * cols] = high

    for z_at in range(full_z):
        store_split(z_at, field_a[HALO + z_at, y0 : y0 + full_y, :])

    def advance(tick, state, older):
        weights = jnp.concatenate([base_ref[2 * cols : 3 * cols], inject_ref[tick]], axis=0)
        inline_ref[...] = jnp.dot(
            split_ref[:, 0 : 2 * cols], base_ref[0 : 2 * cols], preferred_element_type=f32
        ) + jnp.dot(split_ref[:, cols : 3 * cols], weights, preferred_element_type=f32)
        for z_at in range(full_z):
            total = inline_ref[z_at * full_y : (z_at + 1) * full_y]
            z_in = HALO + z_at
            centre = state[z_in, y0 : y0 + full_y, :]
            for distance in range(1, 5):
                pairs = state[z_in - distance, y0 : y0 + full_y, :] + state[z_in + distance, y0 : y0 + full_y, :]
                pairs = pairs + (
                    state[z_in, y0 - distance : y0 - distance + full_y, :]
                    + state[z_in, y0 + distance : y0 + distance + full_y, :]
                )
                total = total + STENCIL_WEIGHTS[distance] * pairs
            updated = (2.0 * centre - older[z_in, y0 : y0 + full_y, :]) + speed_ref[z_at] * total
            older[z_in, y0 : y0 + full_y, :] = updated
            store_split(z_at, updated)

    partner_role = 2 * column + 1 - core
    deep = depth + 2

    def snap_copy(snapshot):
        return pltpu.make_async_remote_copy(
            src_ref=stage_ref.at[snapshot],
            dst_ref=snap_ref.at[snapshot, core],
            send_sem=snap_send.at[snapshot],
            recv_sem=snap_recv.at[snapshot],
            device_id=partner,
            device_id_type=MESH,
        )

    def one_image(snapshot, carry):
        @pl.when((snapshot == IMAGES // 2) & (core == 1))
        def _():
            for part in range(2):
                lend_copy(part).wait_recv()

        for pair in range(SUB // 2):
            advance(SUB * snapshot + 2 * pair, field_a, field_b)
            advance(SUB * snapshot + 2 * pair + 1, field_b, field_a)
        stage_ref[snapshot] = field_a[pl.ds(HALO - 1 + depth * partner_role, deep), own_y, :]
        snap_copy(snapshot).start()
        snap_ref[snapshot, core] = field_a[pl.ds(HALO - 1 + depth * role, deep), own_y, :]
        return carry

    lax.fori_loop(0, IMAGES, one_image, 0)
    for snapshot in range(IMAGES):
        snap_copy(snapshot).wait()
    src_out_ref[...] = snap_ref[IMAGES - 1, 0, 1 : 1 + depth]
    rec_out_ref[...] = snap_ref[IMAGES - 1, 1, 1 : 1 + depth]

    def one_lag(slot, carry):
        lag = lags_ref[slot]
        back = jnp.where(lag > 0, cols - 2 * lag, -2 * lag)
        shift = jnp.where(lag < 0, cols + lag, lag)
        summed = jnp.zeros((deep * rows, cols), f32)
        for snapshot in range(IMAGES):
            moved = pltpu.roll(snap_ref[snapshot, 1].reshape(deep * rows, cols), back, 1)
            summed = summed + snap_ref[snapshot, 0].reshape(deep * rows, cols) * moved
        filtered = (
            2.0 * summed[rows : rows + cells] - summed[0:cells] - summed[2 * rows : 2 * rows + cells]
        )
        filtered = pltpu.roll(filtered, shift, 1)
        lane = lax.broadcasted_iota(jnp.int32, (cells, cols), 1)
        reach = jnp.abs(lag)
        inside = (lane >= reach) & (lane < cols - reach)
        image_ref[slot] = jnp.where(inside, filtered, 0.0).reshape(depth, rows, cols)
        return carry

    lax.fori_loop(0, lags_ref.shape[0], one_lag, 0, unroll=8)
    @pl.when(core == 0)
    def _():
        for part in range(2):
            lend_copy(part).wait_send()

    for copy in sends:
        copy.wait_send()


def window_shards(bands, roles, *arrays):
    rec_pos, rec_traces, offset_lags = arrays[8:]
    depth, rows, cols = arrays[0].shape
    cells = depth * rows
    full_z, full_y = depth * roles, rows * bands
    lag_count = offset_lags.shape[0]
    columns = roles // 2
    steps = SUB * IMAGES
    f32, bf16 = jnp.float32, jnp.bfloat16
    vmem = pl.BlockSpec(memory_space=pltpu.VMEM)
    hbm = pl.BlockSpec(memory_space=pltpu.HBM)
    arrays = arrays[:8] + (rec_pos.T, rec_traces.T, offset_lags)
    places = [pltpu.SMEM if at in (1, 6, 7, 10) else pltpu.VMEM for at in range(len(arrays))]
    padded = (full_z + 2 * HALO, full_y + 16, cols)
    image, source, receiver = pl.pallas_call(
        functools.partial(window_kernel, bands, roles),
        out_shape=(
            jax.ShapeDtypeStruct((lag_count, depth, rows, cols), f32),
            jax.ShapeDtypeStruct((depth, rows, cols), f32),
            jax.ShapeDtypeStruct((depth, rows, cols), f32),
        ),
        in_specs=[hbm] * len(arrays),
        out_specs=(vmem, vmem, vmem),
        scratch_shapes=[place(array.shape, array.dtype) for place, array in zip(places, arrays)]
        + [
            pltpu.VMEM((2, 3 * cells, cols), WIRE),
            pltpu.VMEM((bands * roles, 3 * cells, cols), WIRE),
            pltpu.VMEM(padded, f32),
            pltpu.VMEM(padded, f32),
            pltpu.VMEM((full_z, full_y, cols), f32),
            pltpu.VMEM((full_z * full_y, 3 * cols), bf16),
            pltpu.VMEM((full_z * full_y, cols), f32),
            pltpu.VMEM((3 * cols, cols), bf16),
            pltpu.VMEM((steps, cols, cols), bf16),
            pltpu.VMEM((IMAGES, depth + 2, rows, cols), f32),
            pltpu.VMEM((IMAGES, 2, depth + 2, rows, cols), f32),
            pltpu.SemaphoreType.DMA((2 * bands,)),
            pltpu.SemaphoreType.DMA((2 * bands * columns,)),
            pltpu.SemaphoreType.DMA((bands * roles,)),
            pltpu.SemaphoreType.DMA((IMAGES,)),
            pltpu.SemaphoreType.DMA((IMAGES,)),
            pltpu.VMEM((2, steps // 2, full_y, cols), bf16),
            pltpu.SemaphoreType.DMA((len(arrays),)),
            pltpu.SemaphoreType.DMA((2,)),
            pltpu.SemaphoreType.DMA((2,)),
        ],
        compiler_params=pltpu.CompilerParams(
            collective_id=0, has_side_effects=True, vmem_limit_bytes=48 * 1024 * 1024
        ),
    )(*arrays)
    return image.astype(bf16), source, receiver


def shards(bands, roles, *arrays):
    depth, rows, cols = arrays[0].shape
    sources = arrays[6].shape[0]
    small = depth * roles * rows * bands * cols <= WINDOW_CELLS
    fits = roles % 2 == 0 and rows % 8 == 0 and cols % 128 == 0
    fits = fits and max(rows * bands, sources) <= cols // 2 and arrays[10].shape[0] < cols
    fits = fits and (depth * rows) % 16 == 0 and arrays[1].shape[0] <= 256
    if small and fits:
        return window_shards(bands, roles, *arrays)
    return tile_shards(*arrays)


def solution(mesh):
    placed = (
        P("role", "band", None),
        P(),
        P(("survey", "role"), "band", None),
        P(("survey", "role"), "band", None),
        P(("survey", "role"), "band", None),
        P(("survey", "role"), "band", None),
        P("survey", None),
        P("survey", None),
        P("survey", None),
        P("survey", None),
        P(),
    )
    return jax.shard_map(
        functools.partial(shards, mesh.shape["band"], mesh.shape["role"]),
        mesh=mesh,
        in_specs=placed,
        out_specs=(
            P("survey", "role", "band", None),
            P(("survey", "role"), "band", None),
            P(("survey", "role"), "band", None),
        ),
        check_vma=False,
    )
```

```python
import functools

import jax
import jax.numpy as jnp
from jax import lax
from jax.experimental import pallas as pl
from jax.experimental.pallas import tpu as pltpu
from jax.sharding import PartitionSpec as P

SUB = 4
IMAGES = 4
HALO = 4
WINDOW_CELLS = 1 << 17
MESH = pl.DeviceIdType.MESH
WIRE = jnp.bfloat16
VMEM_GRANT = 64 * 1024 * 1024


STENCIL_WEIGHTS = (-205.0 / 72.0, 8.0 / 5.0, -1.0 / 5.0, 8.0 / 315.0, -1.0 / 560.0)


def padded_2(block, sides, width):
    for axis, dim in sides:
        count = lax.axis_size(axis)
        forward = [(i, i + 1) for i in range(count - 1)]
        backward = [(target, source) for source, target in forward]
        low = lax.ppermute(
            lax.slice_in_dim(block, block.shape[dim] - width, None, axis=dim), axis, forward
        )
        high = lax.ppermute(lax.slice_in_dim(block, 0, width, axis=dim), axis, backward)
        block = jnp.concatenate([low, block, high], axis=dim)
    return block


def laplace(padded, depth_cells, row_cells, col_cells):

    def window(along_z, along_y, along_x):
        return padded[
            :,
            4 + along_z : 4 + along_z + depth_cells,
            4 + along_y : 4 + along_y + row_cells,
            4 + along_x : 4 + along_x + col_cells,
        ]

    summed = 3.0 * STENCIL_WEIGHTS[0] * window(0, 0, 0)
    for distance in range(1, 5):
        weight = STENCIL_WEIGHTS[distance]
        pairs = window(distance, 0, 0) + window(-distance, 0, 0)
        pairs = pairs + window(0, distance, 0) + window(0, -distance, 0)
        pairs = pairs + window(0, 0, distance) + window(0, 0, -distance)
        summed = summed + weight * pairs
    return summed


def lookup(vel_index, courant):
    levels = courant.shape[0]

    def add_level(level, summed):
        return summed + jnp.where(vel_index == level, courant[level], 0.0)

    return lax.fori_loop(0, levels, add_level, jnp.zeros(vel_index.shape, jnp.float32))


def local_index(global_at, start, extent):
    local_at = global_at - start
    inside = (local_at >= 0) & (local_at < extent)
    return jnp.where(inside, local_at, extent)


def inject_all(shape, depth_at, row_at, col_at, amounts):
    step_count = amounts.shape[1]
    return (
        jnp.zeros((step_count,) + shape, jnp.float32)
        .at[:, depth_at, row_at, col_at]
        .add(amounts.T, mode="drop")
    )


def lag_products(source_pad, receiver_pad, offset_lags, max_lag, col_cells):

    def product(lag_value):
        src_part = lax.dynamic_slice_in_dim(source_pad, max_lag - lag_value, col_cells, 2)
        rec_part = lax.dynamic_slice_in_dim(receiver_pad, max_lag + lag_value, col_cells, 2)
        return src_part * rec_part

    return jax.vmap(product)(offset_lags)


def depth_filter(padded, depth_cells):
    return (
        2.0 * padded[:, 1 : 1 + depth_cells]
        - padded[:, 0:depth_cells]
        - padded[:, 2 : 2 + depth_cells]
    )


def pad_inline(state, max_lag):
    return jnp.pad(state, ((0, 0), (0, 0), (0, 0), (max_lag, max_lag)))


def accumulate(slab_state, image_sum, edge_sum, offset_lags, max_lag):
    col_cells = slab_state.shape[3]
    padded = pad_inline(slab_state, max_lag)
    image_sum = image_sum + lag_products(padded[0], padded[1], offset_lags, max_lag, col_cells)
    return (image_sum, edge_sum)


def finish(image_sum):
    padded = padded_2(image_sum, (("role", 1),), 1)
    return depth_filter(padded, image_sum.shape[1]).astype(jnp.bfloat16)


def tile_shards(
    vel_index,
    courant,
    src_now,
    src_prev,
    rec_now,
    rec_prev,
    src_pos,
    src_wavelet,
    rec_pos,
    rec_traces,
    offset_lags,
):
    lag_count = offset_lags.shape[0]
    max_lag = lag_count // 2
    speed = lookup(vel_index, courant)
    band_start = lax.axis_index("band") * src_now.shape[1]
    role_at = lax.axis_index("role")
    current = jnp.stack([src_now, rec_now])
    previous = jnp.stack([src_prev, rec_prev])
    depth_start = role_at * src_now.shape[0]
    col_start = 0

    def faces(state):
        padded = padded_2(state, (("band", 2), ("role", 1)), 4)
        return jnp.pad(padded, ((0, 0), (0, 0), (0, 0), (4, 4)))

    depth_cells, row_cells, col_cells = speed.shape
    shape = speed.shape
    slab_shape = src_now.shape
    src_depth = local_index(src_pos[:, 0], depth_start, depth_cells)
    src_row = local_index(src_pos[:, 1], band_start, row_cells)
    src_col = local_index(src_pos[:, 2], col_start, col_cells)
    rec_depth = local_index(jnp.zeros_like(rec_pos[:, 0]), depth_start, depth_cells)
    rec_row = local_index(rec_pos[:, 0], band_start, row_cells)
    rec_col = local_index(rec_pos[:, 1], col_start, col_cells)
    src_terms = inject_all(shape, src_depth, src_row, src_col, src_wavelet)
    rec_terms = inject_all(shape, rec_depth, rec_row, rec_col, rec_traces)
    image_sum = jnp.zeros((lag_count,) + slab_shape, jnp.float32)
    edge_sum = jnp.zeros((lag_count, 2) + slab_shape[1:], jnp.float32)
    slab_state = current
    for snapshot in range(IMAGES):

        def advance(substep, carry):
            state, older = carry
            tick_at = snapshot * SUB + substep
            sources = jnp.stack(
                [
                    lax.dynamic_index_in_dim(src_terms, tick_at, 0, keepdims=False),
                    lax.dynamic_index_in_dim(rec_terms, tick_at, 0, keepdims=False),
                ]
            )
            laplacian = laplace(faces(state), depth_cells, row_cells, col_cells)
            updated = 2.0 * state - older + speed * (laplacian + sources)
            return (updated, state)

        current, previous = lax.fori_loop(0, SUB, advance, (current, previous))
        slab_state = current
        image_sum, edge_sum = accumulate(slab_state, image_sum, edge_sum, offset_lags, max_lag)
    image = finish(image_sum)
    return (image, slab_state[0], slab_state[1])


def split_two(value):
    high = value.astype(jnp.bfloat16)
    low = (value - high.astype(jnp.float32)).astype(jnp.bfloat16)
    return high, low


def inline_matrix(cols):
    row = lax.broadcasted_iota(jnp.int32, (cols, cols), 0)
    col = lax.broadcasted_iota(jnp.int32, (cols, cols), 1)
    apart = jnp.abs(row - col)
    matrix = jnp.where(apart == 0, 3.0 * STENCIL_WEIGHTS[0], 0.0)
    for distance in range(1, 5):
        matrix = jnp.where(apart == distance, STENCIL_WEIGHTS[distance], matrix)
    return matrix


def window_kernel(
    bands,
    roles,
    *refs,
):
    inputs, outputs, held = refs[:11], refs[11:14], refs[14:25]
    (
        vel_ref,
        courant_ref,
        src_now_ref,
        src_prev_ref,
        rec_now_ref,
        rec_prev_ref,
        src_pos_ref,
        src_wave_ref,
        rec_pos_ref,
        rec_trace_ref,
        lags_ref,
    ) = held
    image_ref, src_out_ref, rec_out_ref = outputs
    (
        out_buf,
        blocks,
        field_a,
        field_b,
        speed_ref,
        split_ref,
        inline_ref,
        base_ref,
        inject_ref,
        stage_ref,
        snap_ref,
        near_send,
        far_send,
        block_recv,
        snap_send,
        snap_recv,
        lend_ref,
        image_buf,
        out_sem,
        in_sem,
        lend_send,
        lend_recv,
    ) = refs[25:]
    fetches = [
        pltpu.make_async_copy(given, kept, in_sem.at[at])
        for at, (given, kept) in enumerate(zip(inputs, held))
    ]
    for fetch in fetches:
        fetch.start()
    inject_ref[...] = jnp.zeros_like(inject_ref)
    depth, rows, cols = vel_ref.shape
    full_z, full_y = depth * roles, rows * bands
    cells = depth * rows
    columns = roles // 2
    survey = lax.axis_index("survey")
    band = lax.axis_index("band")
    role = lax.axis_index("role")
    core = lax.rem(role, 2)
    column = role // 2
    own = band * roles + role
    f32 = jnp.float32
    y0 = 8

    def device(at_band, at_role):
        return (survey, at_band, at_role)

    partner = device(band, 2 * column + 1 - core)
    barrier = pltpu.get_barrier_semaphore()
    greeted = 0
    for step in range(1, bands):
        for side in range(2):
            pl.semaphore_signal(
                barrier,
                inc=1,
                device_id=device(lax.rem(band + step, bands), 2 * column + side),
                device_id_type=MESH,
            )
            greeted += 1
    pl.semaphore_signal(barrier, inc=1, device_id=partner, device_id_type=MESH)
    greeted += 1
    for step in range(1, columns):
        pl.semaphore_signal(
            barrier,
            inc=1,
            device_id=device(band, 2 * lax.rem(column + step, columns) + core),
            device_id_type=MESH,
        )
        greeted += 1

    for at in (0, 2, 3, 4, 5):
        fetches[at].wait()
    index = vel_ref[...].astype(f32).reshape(cells, cols)
    for side, now_ref, prev_ref in ((0, src_now_ref, src_prev_ref), (1, rec_now_ref, rec_prev_ref)):
        now = now_ref[...].reshape(cells, cols)
        change = now - prev_ref[...].reshape(cells, cols)
        out_buf[side, 0:cells] = now.astype(WIRE)
        out_buf[side, cells : 2 * cells] = change.astype(WIRE)
        out_buf[side, 2 * cells : 3 * cells] = index.astype(WIRE)
    pl.semaphore_wait(barrier, greeted)

    sends = []
    for step in range(1, bands):
        for side in range(2):
            copy = pltpu.make_async_remote_copy(
                src_ref=out_buf.at[side],
                dst_ref=blocks.at[own],
                send_sem=near_send.at[2 * step + side],
                recv_sem=block_recv.at[own],
                device_id=device(lax.rem(band + step, bands), 2 * column + side),
                device_id_type=MESH,
            )
            copy.start()
            sends.append(copy)
    copy = pltpu.make_async_remote_copy(
        src_ref=out_buf.at[1 - core],
        dst_ref=blocks.at[own],
        send_sem=near_send.at[0],
        recv_sem=block_recv.at[own],
        device_id=partner,
        device_id_type=MESH,
    )
    copy.start()
    sends.append(copy)

    def pass_on(step, source, slot, lane):
        copy = pltpu.make_async_remote_copy(
            src_ref=source,
            dst_ref=blocks.at[slot],
            send_sem=far_send.at[lane],
            recv_sem=block_recv.at[slot],
            device_id=device(band, 2 * lax.rem(column + step, columns) + core),
            device_id_type=MESH,
        )
        copy.start()
        sends.append(copy)

    def landed(slot):
        pltpu.make_async_copy(blocks.at[slot], blocks.at[slot], block_recv.at[slot]).wait()

    for step in range(1, columns):
        pass_on(step, out_buf.at[core], own, step)

    for at in (1, 6, 7, 8, 9, 10):
        fetches[at].wait()
    lines = split_ref.shape[0]
    half = cols // 2
    row_at = lax.broadcasted_iota(jnp.int32, (lines, cols), 0)
    lane_at = lax.broadcasted_iota(jnp.int32, (lines, cols), 1)
    lane_low = jnp.where(lane_at >= half, lane_at - half, lane_at)
    steps = inject_ref.shape[0]

    @pl.when(core == 0)
    def _():
        count = src_pos_ref.shape[0]
        target = jnp.full((1, cols), -1, jnp.int32)
        lane = lax.broadcasted_iota(jnp.int32, (1, cols), 1)
        lane = jnp.where(lane >= half, lane - half, lane)
        for source in range(count):
            line = src_pos_ref[source, 0] * full_y + src_pos_ref[source, 1]
            target = jnp.where(lane == source, line, target)
        split_ref[:, 2 * cols : 3 * cols] = jnp.where(row_at == target, 1.0, 0.0).astype(jnp.bfloat16)
        height = -(-count // 16) * 16
        row = lax.broadcasted_iota(jnp.int32, (height, cols), 0)
        col = lax.broadcasted_iota(jnp.int32, (height, cols), 1)
        for tick in range(steps):
            term = jnp.zeros((height, cols), f32)
            for source in range(count):
                here = (row == source) & (col == src_pos_ref[source, 2])
                term = jnp.where(here, src_wave_ref[source, tick], term)
            high, low = split_two(term)
            inject_ref[tick, 0:height] = high
            inject_ref[tick, half : half + height] = low

    high, low = split_two(inline_matrix(cols))
    base_ref[0:cols] = high
    base_ref[cols : 2 * cols] = high
    base_ref[2 * cols : 3 * cols] = low
    field_a[...] = jnp.zeros_like(field_a)
    field_b[...] = jnp.zeros_like(field_b)

    @pl.when(core == 1)
    def _():
        split_ref[:, 2 * cols : 3 * cols] = jnp.where(
            (row_at < full_y) & (row_at == lane_low), 1.0, 0.0
        ).astype(jnp.bfloat16)

    share = steps // 2
    first = pl.multiple_of(share * (1 - core), share)
    count = rec_pos_ref.shape[1]
    chunk = min(512, count)

    def add_receivers(total, start, stop):
        for at in range(start, stop, chunk):
            size = min(chunk, stop - at)
            y_at = rec_pos_ref[0:1, at : at + size]
            x_at = rec_pos_ref[1:2, at : at + size]
            in_row = lax.broadcasted_iota(jnp.int32, (full_y, size), 0) == y_at
            in_col = lax.broadcasted_iota(jnp.int32, (cols, size), 0) == x_at
            in_col = jnp.where(in_col, 1.0, 0.0).astype(jnp.bfloat16)
            amounts = rec_trace_ref[pl.ds(first, share), at : at + size]
            high = amounts.astype(jnp.bfloat16).astype(f32)
            parts = []
            for part in (high, amounts - high):
                for tick in range(share):
                    parts.append(jnp.where(in_row, part[tick : tick + 1], 0.0).astype(jnp.bfloat16))
            total = total + lax.dot_general(
                jnp.concatenate(parts, axis=0),
                in_col,
                (((1,), (1,)), ((), ())),
                preferred_element_type=f32,
            )
        return total

    middle = count // 2 // chunk * chunk
    added = add_receivers(jnp.zeros((2 * share * full_y, cols), f32), 0, middle)

    slot = band * roles + 2 * column + 1 - core
    landed(slot)
    for step in range(1, columns):
        pass_on(step, blocks.at[slot], slot, columns + step)
    for hop in range(1, bands):
        for side in range(2):
            slot = lax.rem(band + hop, bands) * roles + 2 * column + side
            landed(slot)
            for step in range(1, columns):
                pass_on(step, blocks.at[slot], slot, (2 * hop + side) * columns + step)
    added = add_receivers(added, middle, count)
    size = share * full_y
    high, low = split_two(added[0:size] + added[size : 2 * size])
    lend_ref[0] = high.reshape(share, full_y, cols)
    lend_ref[1] = low.reshape(share, full_y, cols)

    def lend_copy(part):
        return pltpu.make_async_remote_copy(
            src_ref=lend_ref.at[part],
            dst_ref=inject_ref.at[pl.ds(share, share), pl.ds(part * half, full_y)],
            send_sem=lend_send.at[part],
            recv_sem=lend_recv.at[part],
            device_id=partner,
            device_id_type=MESH,
        )

    @pl.when(core == 0)
    def _():
        for part in range(2):
            lend_copy(part).start()

    @pl.when(core == 1)
    def _():
        for part in range(2):
            inject_ref[0:share, part * half : part * half + full_y] = lend_ref[part]

    def table(values):
        found = jnp.zeros(values.shape, f32)
        for level in range(courant_ref.shape[0]):
            found = jnp.where(values == float(level), courant_ref[level], found)
        return found

    def unpack(at_band, at_role, block):
        now = block[0:cells].reshape(depth, rows, cols)
        prev = now - block[cells : 2 * cells].reshape(depth, rows, cols)
        z_part = pl.ds(HALO + depth * at_role, depth)
        y_part = pl.ds(pl.multiple_of(y0 + rows * at_band, rows), rows)
        field_a[z_part, y_part, :] = now
        field_b[z_part, y_part, :] = prev
        speed_ref[pl.ds(depth * at_role, depth), pl.ds(pl.multiple_of(rows * at_band, rows), rows), :] = table(
            block[2 * cells : 3 * cells]
        ).reshape(depth, rows, cols)

    for hop in range(bands):
        for side in range(2):
            at_band, at_role = lax.rem(band + hop, bands), 2 * column + lax.rem(core + side, 2)
            if hop == 0 and side == 0:
                unpack(band, role, out_buf[core].astype(f32))
            else:
                unpack(at_band, at_role, blocks[at_band * roles + at_role].astype(f32))
    for hop in range(bands):
        for step in range(1, columns):
            for side in range(2):
                at_band = lax.rem(band + hop, bands)
                at_role = 2 * lax.rem(column + step, columns) + lax.rem(core + side, 2)
                landed(at_band * roles + at_role)
                unpack(at_band, at_role, blocks[at_band * roles + at_role].astype(f32))

    own_z = pl.ds(HALO + depth * role, depth)
    own_y = pl.ds(pl.multiple_of(y0 + rows * band, rows), rows)
    field_a[own_z, own_y, :] = jnp.where(core == 0, src_now_ref[...], rec_now_ref[...])
    field_b[own_z, own_y, :] = jnp.where(core == 0, src_prev_ref[...], rec_prev_ref[...])

    def store_split(z_at, value):
        high, low = split_two(value)
        split_ref[pl.ds(z_at * full_y, full_y), 0:cols] = low
        split_ref[pl.ds(z_at * full_y, full_y), cols : 2 * cols] = high

    for z_at in range(full_z):
        store_split(z_at, field_a[HALO + z_at, y0 : y0 + full_y, :])

    def advance(tick, state, older):
        weights = jnp.concatenate([base_ref[2 * cols : 3 * cols], inject_ref[tick]], axis=0)
        inline_ref[...] = jnp.dot(
            split_ref[:, 0 : 2 * cols], base_ref[0 : 2 * cols], preferred_element_type=f32
        ) + jnp.dot(split_ref[:, cols : 3 * cols], weights, preferred_element_type=f32)
        for z_at in range(full_z):
            total = inline_ref[z_at * full_y : (z_at + 1) * full_y]
            z_in = HALO + z_at
            centre = state[z_in, y0 : y0 + full_y, :]
            for distance in range(1, 5):
                pairs = state[z_in - distance, y0 : y0 + full_y, :] + state[z_in + distance, y0 : y0 + full_y, :]
                pairs = pairs + (
                    state[z_in, y0 - distance : y0 - distance + full_y, :]
                    + state[z_in, y0 + distance : y0 + distance + full_y, :]
                )
                total = total + STENCIL_WEIGHTS[distance] * pairs
            updated = (2.0 * centre - older[z_in, y0 : y0 + full_y, :]) + speed_ref[z_at] * total
            older[z_in, y0 : y0 + full_y, :] = updated
            store_split(z_at, updated)

    partner_role = 2 * column + 1 - core
    deep = depth + 2

    def snap_copy(snapshot):
        return pltpu.make_async_remote_copy(
            src_ref=stage_ref.at[snapshot],
            dst_ref=snap_ref.at[snapshot, core],
            send_sem=snap_send.at[snapshot],
            recv_sem=snap_recv.at[snapshot],
            device_id=partner,
            device_id_type=MESH,
        )

    def one_image(snapshot, carry):
        @pl.when((snapshot == IMAGES // 2) & (core == 1))
        def _():
            for part in range(2):
                lend_copy(part).wait_recv()

        for pair in range(SUB // 2):
            advance(SUB * snapshot + 2 * pair, field_a, field_b)
            advance(SUB * snapshot + 2 * pair + 1, field_b, field_a)
        stage_ref[snapshot] = field_a[pl.ds(HALO - 1 + depth * partner_role, deep), own_y, :]
        snap_copy(snapshot).start()
        snap_ref[snapshot, core] = field_a[pl.ds(HALO - 1 + depth * role, deep), own_y, :]
        return carry

    lax.fori_loop(0, IMAGES, one_image, 0)
    for snapshot in range(IMAGES):
        snap_copy(snapshot).wait()
    results = [
        pltpu.make_async_copy(snap_ref.at[IMAGES - 1, side, pl.ds(1, depth)], kept, out_sem.at[side])
        for side, kept in enumerate((src_out_ref, rec_out_ref))
    ]
    for result in results:
        result.start()

    def one_lag(slot, carry):
        lag = lags_ref[slot]
        back = jnp.where(lag > 0, cols - 2 * lag, -2 * lag)
        shift = jnp.where(lag < 0, cols + lag, lag)
        summed = jnp.zeros((deep * rows, cols), f32)
        for snapshot in range(IMAGES):
            moved = pltpu.roll(snap_ref[snapshot, 1].reshape(deep * rows, cols), back, 1)
            summed = summed + snap_ref[snapshot, 0].reshape(deep * rows, cols) * moved
        filtered = (
            2.0 * summed[rows : rows + cells] - summed[0:cells] - summed[2 * rows : 2 * rows + cells]
        )
        filtered = pltpu.roll(filtered, shift, 1)
        lane = lax.broadcasted_iota(jnp.int32, (cells, cols), 1)
        reach = jnp.abs(lag)
        inside = (lane >= reach) & (lane < cols - reach)
        at = pl.multiple_of(slot * cells, cells)
        image_buf[pl.ds(at, cells)] = jnp.where(inside, filtered, 0.0).astype(jnp.bfloat16)
        return carry

    lag_count = lags_ref.shape[0]
    group = -(-lag_count // 4)
    for turn, start in enumerate(range(0, lag_count, group)):
        stop = min(start + group, lag_count)
        lax.fori_loop(start, stop, one_lag, 0, unroll=group)
        part = pl.ds(start * cells, (stop - start) * cells)
        result = pltpu.make_async_copy(image_buf.at[part], image_ref.at[part], out_sem.at[2 + turn])
        result.start()
        results.append(result)
    for result in results:
        result.wait()
    @pl.when(core == 0)
    def _():
        for part in range(2):
            lend_copy(part).wait_send()

    for copy in sends:
        copy.wait_send()


def hand_over(*refs):
    copies = [pltpu.make_async_copy(refs[at], refs[3 + at], refs[6].at[at]) for at in range(3)]
    for copy in copies:
        copy.start()
    for copy in copies:
        copy.wait()


def window_shards(bands, roles, *arrays):
    rec_pos, rec_traces, offset_lags = arrays[8:]
    depth, rows, cols = arrays[0].shape
    cells = depth * rows
    full_z, full_y = depth * roles, rows * bands
    lag_count = offset_lags.shape[0]
    columns = roles // 2
    steps = SUB * IMAGES
    f32, bf16 = jnp.float32, jnp.bfloat16
    hbm = pl.BlockSpec(memory_space=pltpu.HBM)
    arrays = arrays[:8] + (rec_pos.T, rec_traces.T, offset_lags)
    places = [pltpu.SMEM if at in (1, 6, 7, 10) else pltpu.VMEM for at in range(len(arrays))]
    padded = (full_z + 2 * HALO, full_y + 16, cols)
    results = pl.pallas_call(
        functools.partial(window_kernel, bands, roles),
        out_shape=(
            jax.ShapeDtypeStruct((lag_count * cells, cols), bf16),
            jax.ShapeDtypeStruct((depth, rows, cols), f32),
            jax.ShapeDtypeStruct((depth, rows, cols), f32),
        ),
        in_specs=[hbm] * len(arrays),
        out_specs=(hbm, hbm, hbm),
        scratch_shapes=[place(array.shape, array.dtype) for place, array in zip(places, arrays)]
        + [
            pltpu.VMEM((2, 3 * cells, cols), WIRE),
            pltpu.VMEM((bands * roles, 3 * cells, cols), WIRE),
            pltpu.VMEM(padded, f32),
            pltpu.VMEM(padded, f32),
            pltpu.VMEM((full_z, full_y, cols), f32),
            pltpu.VMEM((full_z * full_y, 3 * cols), bf16),
            pltpu.VMEM((full_z * full_y, cols), f32),
            pltpu.VMEM((3 * cols, cols), bf16),
            pltpu.VMEM((steps, cols, cols), bf16),
            pltpu.VMEM((IMAGES, depth + 2, rows, cols), f32),
            pltpu.VMEM((IMAGES, 2, depth + 2, rows, cols), f32),
            pltpu.SemaphoreType.DMA((2 * bands,)),
            pltpu.SemaphoreType.DMA((2 * bands * columns,)),
            pltpu.SemaphoreType.DMA((bands * roles,)),
            pltpu.SemaphoreType.DMA((IMAGES,)),
            pltpu.SemaphoreType.DMA((IMAGES,)),
            pltpu.VMEM((2, steps // 2, full_y, cols), bf16),
            pltpu.VMEM((lag_count * cells, cols), bf16),
            pltpu.SemaphoreType.DMA((6,)),
            pltpu.SemaphoreType.DMA((len(arrays),)),
            pltpu.SemaphoreType.DMA((2,)),
            pltpu.SemaphoreType.DMA((2,)),
        ],
        compiler_params=pltpu.CompilerParams(
            collective_id=0, has_side_effects=True, vmem_limit_bytes=VMEM_GRANT
        ),
    )(*arrays)
    image, source, receiver = pl.pallas_call(
        hand_over,
        out_shape=tuple(jax.ShapeDtypeStruct(result.shape, result.dtype) for result in results),
        in_specs=[hbm] * 3,
        out_specs=(hbm, hbm, hbm),
        scratch_shapes=[pltpu.SemaphoreType.DMA((3,))],
        compiler_params=pltpu.CompilerParams(vmem_limit_bytes=VMEM_GRANT),
    )(*results)
    return image.reshape(lag_count, depth, rows, cols), source, receiver


def shards(bands, roles, *arrays):
    depth, rows, cols = arrays[0].shape
    sources = arrays[6].shape[0]
    small = depth * roles * rows * bands * cols <= WINDOW_CELLS
    fits = roles % 2 == 0 and rows % 8 == 0 and cols % 128 == 0
    fits = fits and max(rows * bands, sources) <= cols // 2 and arrays[10].shape[0] < cols
    fits = fits and (depth * rows) % 16 == 0 and arrays[1].shape[0] <= 256
    if small and fits:
        return window_shards(bands, roles, *arrays)
    return tile_shards(*arrays)


def solution(mesh):
    placed = (
        P("role", "band", None),
        P(),
        P(("survey", "role"), "band", None),
        P(("survey", "role"), "band", None),
        P(("survey", "role"), "band", None),
        P(("survey", "role"), "band", None),
        P("survey", None),
        P("survey", None),
        P("survey", None),
        P("survey", None),
        P(),
    )
    return jax.shard_map(
        functools.partial(shards, mesh.shape["band"], mesh.shape["role"]),
        mesh=mesh,
        in_specs=placed,
        out_specs=(
            P("survey", "role", "band", None),
            P(("survey", "role"), "band", None),
            P(("survey", "role"), "band", None),
        ),
        check_vma=False,
    )
```

```python
import functools

import jax
import jax.numpy as jnp
from jax import lax
from jax.experimental import pallas as pl
from jax.experimental.pallas import tpu as pltpu
from jax.sharding import PartitionSpec as P

SUB = 4
IMAGES = 4
HALO = 4
WINDOW_CELLS = 1 << 17
MESH = pl.DeviceIdType.MESH
LAYERS = 4
WIRE = jnp.bfloat16
VMEM_GRANT = 64 * 1024 * 1024


STENCIL_WEIGHTS = (-205.0 / 72.0, 8.0 / 5.0, -1.0 / 5.0, 8.0 / 315.0, -1.0 / 560.0)


def padded_2(block, sides, width):
    for axis, dim in sides:
        count = lax.axis_size(axis)
        forward = [(i, i + 1) for i in range(count - 1)]
        backward = [(target, source) for source, target in forward]
        low = lax.ppermute(
            lax.slice_in_dim(block, block.shape[dim] - width, None, axis=dim), axis, forward
        )
        high = lax.ppermute(lax.slice_in_dim(block, 0, width, axis=dim), axis, backward)
        block = jnp.concatenate([low, block, high], axis=dim)
    return block


def laplace(padded, depth_cells, row_cells, col_cells):

    def window(along_z, along_y, along_x):
        return padded[
            :,
            4 + along_z : 4 + along_z + depth_cells,
            4 + along_y : 4 + along_y + row_cells,
            4 + along_x : 4 + along_x + col_cells,
        ]

    summed = 3.0 * STENCIL_WEIGHTS[0] * window(0, 0, 0)
    for distance in range(1, 5):
        weight = STENCIL_WEIGHTS[distance]
        pairs = window(distance, 0, 0) + window(-distance, 0, 0)
        pairs = pairs + window(0, distance, 0) + window(0, -distance, 0)
        pairs = pairs + window(0, 0, distance) + window(0, 0, -distance)
        summed = summed + weight * pairs
    return summed


def lookup(vel_index, courant):
    levels = courant.shape[0]

    def add_level(level, summed):
        return summed + jnp.where(vel_index == level, courant[level], 0.0)

    return lax.fori_loop(0, levels, add_level, jnp.zeros(vel_index.shape, jnp.float32))


def local_index(global_at, start, extent):
    local_at = global_at - start
    inside = (local_at >= 0) & (local_at < extent)
    return jnp.where(inside, local_at, extent)


def inject_all(shape, depth_at, row_at, col_at, amounts):
    step_count = amounts.shape[1]
    return (
        jnp.zeros((step_count,) + shape, jnp.float32)
        .at[:, depth_at, row_at, col_at]
        .add(amounts.T, mode="drop")
    )


def lag_products(source_pad, receiver_pad, offset_lags, max_lag, col_cells):

    def product(lag_value):
        src_part = lax.dynamic_slice_in_dim(source_pad, max_lag - lag_value, col_cells, 2)
        rec_part = lax.dynamic_slice_in_dim(receiver_pad, max_lag + lag_value, col_cells, 2)
        return src_part * rec_part

    return jax.vmap(product)(offset_lags)


def depth_filter(padded, depth_cells):
    return (
        2.0 * padded[:, 1 : 1 + depth_cells]
        - padded[:, 0:depth_cells]
        - padded[:, 2 : 2 + depth_cells]
    )


def pad_inline(state, max_lag):
    return jnp.pad(state, ((0, 0), (0, 0), (0, 0), (max_lag, max_lag)))


def accumulate(slab_state, image_sum, edge_sum, offset_lags, max_lag):
    col_cells = slab_state.shape[3]
    padded = pad_inline(slab_state, max_lag)
    image_sum = image_sum + lag_products(padded[0], padded[1], offset_lags, max_lag, col_cells)
    return (image_sum, edge_sum)


def finish(image_sum):
    padded = padded_2(image_sum, (("role", 1),), 1)
    return depth_filter(padded, image_sum.shape[1]).astype(jnp.bfloat16)


def tile_shards(
    vel_index,
    courant,
    src_now,
    src_prev,
    rec_now,
    rec_prev,
    src_pos,
    src_wavelet,
    rec_pos,
    rec_traces,
    offset_lags,
):
    lag_count = offset_lags.shape[0]
    max_lag = lag_count // 2
    speed = lookup(vel_index, courant)
    band_start = lax.axis_index("band") * src_now.shape[1]
    role_at = lax.axis_index("role")
    current = jnp.stack([src_now, rec_now])
    previous = jnp.stack([src_prev, rec_prev])
    depth_start = role_at * src_now.shape[0]
    col_start = 0

    def faces(state):
        padded = padded_2(state, (("band", 2), ("role", 1)), 4)
        return jnp.pad(padded, ((0, 0), (0, 0), (0, 0), (4, 4)))

    depth_cells, row_cells, col_cells = speed.shape
    shape = speed.shape
    slab_shape = src_now.shape
    src_depth = local_index(src_pos[:, 0], depth_start, depth_cells)
    src_row = local_index(src_pos[:, 1], band_start, row_cells)
    src_col = local_index(src_pos[:, 2], col_start, col_cells)
    rec_depth = local_index(jnp.zeros_like(rec_pos[:, 0]), depth_start, depth_cells)
    rec_row = local_index(rec_pos[:, 0], band_start, row_cells)
    rec_col = local_index(rec_pos[:, 1], col_start, col_cells)
    src_terms = inject_all(shape, src_depth, src_row, src_col, src_wavelet)
    rec_terms = inject_all(shape, rec_depth, rec_row, rec_col, rec_traces)
    image_sum = jnp.zeros((lag_count,) + slab_shape, jnp.float32)
    edge_sum = jnp.zeros((lag_count, 2) + slab_shape[1:], jnp.float32)
    slab_state = current
    for snapshot in range(IMAGES):

        def advance(substep, carry):
            state, older = carry
            tick_at = snapshot * SUB + substep
            sources = jnp.stack(
                [
                    lax.dynamic_index_in_dim(src_terms, tick_at, 0, keepdims=False),
                    lax.dynamic_index_in_dim(rec_terms, tick_at, 0, keepdims=False),
                ]
            )
            laplacian = laplace(faces(state), depth_cells, row_cells, col_cells)
            updated = 2.0 * state - older + speed * (laplacian + sources)
            return (updated, state)

        current, previous = lax.fori_loop(0, SUB, advance, (current, previous))
        slab_state = current
        image_sum, edge_sum = accumulate(slab_state, image_sum, edge_sum, offset_lags, max_lag)
    image = finish(image_sum)
    return (image, slab_state[0], slab_state[1])


def split_two(value):
    high = value.astype(jnp.bfloat16)
    low = (value - high.astype(jnp.float32)).astype(jnp.bfloat16)
    return high, low


def inline_matrix(cols):
    row = lax.broadcasted_iota(jnp.int32, (cols, cols), 0)
    col = lax.broadcasted_iota(jnp.int32, (cols, cols), 1)
    apart = jnp.abs(row - col)
    matrix = jnp.where(apart == 0, 3.0 * STENCIL_WEIGHTS[0], 0.0)
    for distance in range(1, 5):
        matrix = jnp.where(apart == distance, STENCIL_WEIGHTS[distance], matrix)
    return matrix


def window_kernel(
    bands,
    roles,
    *refs,
):
    inputs, outputs, held = refs[:11], refs[11:14], refs[14:25]
    (
        vel_ref,
        courant_ref,
        src_now_ref,
        src_prev_ref,
        rec_now_ref,
        rec_prev_ref,
        src_pos_ref,
        src_wave_ref,
        rec_pos_ref,
        rec_trace_ref,
        lags_ref,
    ) = held
    image_ref, src_out_ref, rec_out_ref = outputs
    (
        out_buf,
        blocks,
        field_a,
        field_b,
        speed_ref,
        split_ref,
        base_ref,
        inject_ref,
        stage_ref,
        snap_ref,
        near_send,
        far_send,
        block_recv,
        snap_send,
        snap_recv,
        lend_ref,
        image_buf,
        out_sem,
        in_sem,
        lend_send,
        lend_recv,
    ) = refs[25:]
    fetches = [
        pltpu.make_async_copy(given, kept, in_sem.at[at])
        for at, (given, kept) in enumerate(zip(inputs, held))
    ]
    for fetch in fetches:
        fetch.start()
    inject_ref[...] = jnp.zeros_like(inject_ref)
    depth, rows, cols = vel_ref.shape
    full_z, full_y = depth * roles, rows * bands
    cells = depth * rows
    columns = roles // 2
    survey = lax.axis_index("survey")
    band = lax.axis_index("band")
    role = lax.axis_index("role")
    core = lax.rem(role, 2)
    column = role // 2
    own = band * roles + role
    f32 = jnp.float32
    y0 = 8

    def device(at_band, at_role):
        return (survey, at_band, at_role)

    partner = device(band, 2 * column + 1 - core)
    barrier = pltpu.get_barrier_semaphore()
    greeted = 0
    for step in range(1, bands):
        for side in range(2):
            pl.semaphore_signal(
                barrier,
                inc=1,
                device_id=device(lax.rem(band + step, bands), 2 * column + side),
                device_id_type=MESH,
            )
            greeted += 1
    pl.semaphore_signal(barrier, inc=1, device_id=partner, device_id_type=MESH)
    greeted += 1
    for step in range(1, columns):
        pl.semaphore_signal(
            barrier,
            inc=1,
            device_id=device(band, 2 * lax.rem(column + step, columns) + core),
            device_id_type=MESH,
        )
        greeted += 1

    for at in (0, 2, 3, 4, 5):
        fetches[at].wait()
    index = vel_ref[...].astype(f32).reshape(cells, cols)
    for side, now_ref, prev_ref in ((0, src_now_ref, src_prev_ref), (1, rec_now_ref, rec_prev_ref)):
        now = now_ref[...].reshape(cells, cols)
        change = now - prev_ref[...].reshape(cells, cols)
        out_buf[side, 0:cells] = now.astype(WIRE)
        out_buf[side, cells : 2 * cells] = change.astype(WIRE)
        out_buf[side, 2 * cells : 3 * cells] = index.astype(WIRE)
    pl.semaphore_wait(barrier, greeted)

    sends = []
    for step in range(1, bands):
        for side in range(2):
            copy = pltpu.make_async_remote_copy(
                src_ref=out_buf.at[side],
                dst_ref=blocks.at[own],
                send_sem=near_send.at[2 * step + side],
                recv_sem=block_recv.at[own],
                device_id=device(lax.rem(band + step, bands), 2 * column + side),
                device_id_type=MESH,
            )
            copy.start()
            sends.append(copy)
    copy = pltpu.make_async_remote_copy(
        src_ref=out_buf.at[1 - core],
        dst_ref=blocks.at[own],
        send_sem=near_send.at[0],
        recv_sem=block_recv.at[own],
        device_id=partner,
        device_id_type=MESH,
    )
    copy.start()
    sends.append(copy)

    def pass_on(step, source, slot, lane):
        copy = pltpu.make_async_remote_copy(
            src_ref=source,
            dst_ref=blocks.at[slot],
            send_sem=far_send.at[lane],
            recv_sem=block_recv.at[slot],
            device_id=device(band, 2 * lax.rem(column + step, columns) + core),
            device_id_type=MESH,
        )
        copy.start()
        sends.append(copy)

    def landed(slot):
        pltpu.make_async_copy(blocks.at[slot], blocks.at[slot], block_recv.at[slot]).wait()

    for step in range(1, columns):
        pass_on(step, out_buf.at[core], own, step)

    for at in (1, 6, 7, 8, 9, 10):
        fetches[at].wait()
    lines = split_ref.shape[0]
    half = cols // 2
    row_at = lax.broadcasted_iota(jnp.int32, (lines, cols), 0)
    lane_at = lax.broadcasted_iota(jnp.int32, (lines, cols), 1)
    lane_low = jnp.where(lane_at >= half, lane_at - half, lane_at)
    steps = inject_ref.shape[0]

    @pl.when(core == 0)
    def _():
        count = src_pos_ref.shape[0]
        target = jnp.full((1, cols), -1, jnp.int32)
        lane = lax.broadcasted_iota(jnp.int32, (1, cols), 1)
        lane = jnp.where(lane >= half, lane - half, lane)
        for source in range(count):
            line = src_pos_ref[source, 0] * full_y + src_pos_ref[source, 1]
            target = jnp.where(lane == source, line, target)
        split_ref[:, 2 * cols : 3 * cols] = jnp.where(row_at == target, 1.0, 0.0).astype(jnp.bfloat16)
        height = -(-count // 16) * 16
        row = lax.broadcasted_iota(jnp.int32, (height, cols), 0)
        col = lax.broadcasted_iota(jnp.int32, (height, cols), 1)
        for tick in range(steps):
            term = jnp.zeros((height, cols), f32)
            for source in range(count):
                here = (row == source) & (col == src_pos_ref[source, 2])
                term = jnp.where(here, src_wave_ref[source, tick], term)
            high, low = split_two(term)
            inject_ref[tick, 0:height] = high
            inject_ref[tick, half : half + height] = low

    high, low = split_two(inline_matrix(cols))
    base_ref[0:cols] = high
    base_ref[cols : 2 * cols] = high
    base_ref[2 * cols : 3 * cols] = low
    field_a[...] = jnp.zeros_like(field_a)
    field_b[...] = jnp.zeros_like(field_b)

    @pl.when(core == 1)
    def _():
        split_ref[:, 2 * cols : 3 * cols] = jnp.where(
            (row_at < full_y) & (row_at == lane_low), 1.0, 0.0
        ).astype(jnp.bfloat16)

    share = steps // 2
    first = pl.multiple_of(share * (1 - core), share)
    count = rec_pos_ref.shape[1]
    chunk = min(512, count)

    def add_receivers(total, start, stop):
        for at in range(start, stop, chunk):
            size = min(chunk, stop - at)
            y_at = rec_pos_ref[0:1, at : at + size]
            x_at = rec_pos_ref[1:2, at : at + size]
            in_row = lax.broadcasted_iota(jnp.int32, (full_y, size), 0) == y_at
            in_col = lax.broadcasted_iota(jnp.int32, (cols, size), 0) == x_at
            in_col = jnp.where(in_col, 1.0, 0.0).astype(jnp.bfloat16)
            amounts = rec_trace_ref[pl.ds(first, share), at : at + size]
            high = amounts.astype(jnp.bfloat16).astype(f32)
            parts = []
            for part in (high, amounts - high):
                for tick in range(share):
                    parts.append(jnp.where(in_row, part[tick : tick + 1], 0.0).astype(jnp.bfloat16))
            total = total + lax.dot_general(
                jnp.concatenate(parts, axis=0),
                in_col,
                (((1,), (1,)), ((), ())),
                preferred_element_type=f32,
            )
        return total

    middle = count // 2 // chunk * chunk
    added = add_receivers(jnp.zeros((2 * share * full_y, cols), f32), 0, middle)

    slot = band * roles + 2 * column + 1 - core
    landed(slot)
    for step in range(1, columns):
        pass_on(step, blocks.at[slot], slot, columns + step)
    for hop in range(1, bands):
        for side in range(2):
            slot = lax.rem(band + hop, bands) * roles + 2 * column + side
            landed(slot)
            for step in range(1, columns):
                pass_on(step, blocks.at[slot], slot, (2 * hop + side) * columns + step)
    added = add_receivers(added, middle, count)
    size = share * full_y
    high, low = split_two(added[0:size] + added[size : 2 * size])
    lend_ref[0] = high.reshape(share, full_y, cols)
    lend_ref[1] = low.reshape(share, full_y, cols)

    def lend_copy(part):
        return pltpu.make_async_remote_copy(
            src_ref=lend_ref.at[part],
            dst_ref=inject_ref.at[pl.ds(share, share), pl.ds(part * half, full_y)],
            send_sem=lend_send.at[part],
            recv_sem=lend_recv.at[part],
            device_id=partner,
            device_id_type=MESH,
        )

    @pl.when(core == 0)
    def _():
        for part in range(2):
            lend_copy(part).start()

    @pl.when(core == 1)
    def _():
        for part in range(2):
            inject_ref[0:share, part * half : part * half + full_y] = lend_ref[part]

    def table(values):
        found = jnp.zeros(values.shape, f32)
        for level in range(courant_ref.shape[0]):
            found = jnp.where(values == float(level), courant_ref[level], found)
        return found

    def unpack(at_band, at_role, block):
        now = block[0:cells].reshape(depth, rows, cols)
        prev = now - block[cells : 2 * cells].reshape(depth, rows, cols)
        z_part = pl.ds(HALO + depth * at_role, depth)
        y_part = pl.ds(pl.multiple_of(y0 + rows * at_band, rows), rows)
        field_a[z_part, y_part, :] = now
        field_b[z_part, y_part, :] = prev
        speed_ref[pl.ds(depth * at_role, depth), pl.ds(pl.multiple_of(rows * at_band, rows), rows), :] = table(
            block[2 * cells : 3 * cells]
        ).reshape(depth, rows, cols)

    for hop in range(bands):
        for side in range(2):
            at_band, at_role = lax.rem(band + hop, bands), 2 * column + lax.rem(core + side, 2)
            if hop == 0 and side == 0:
                unpack(band, role, out_buf[core].astype(f32))
            else:
                unpack(at_band, at_role, blocks[at_band * roles + at_role].astype(f32))
    for hop in range(bands):
        for step in range(1, columns):
            for side in range(2):
                at_band = lax.rem(band + hop, bands)
                at_role = 2 * lax.rem(column + step, columns) + lax.rem(core + side, 2)
                landed(at_band * roles + at_role)
                unpack(at_band, at_role, blocks[at_band * roles + at_role].astype(f32))

    own_z = pl.ds(HALO + depth * role, depth)
    own_y = pl.ds(pl.multiple_of(y0 + rows * band, rows), rows)
    field_a[own_z, own_y, :] = jnp.where(core == 0, src_now_ref[...], rec_now_ref[...])
    field_b[own_z, own_y, :] = jnp.where(core == 0, src_prev_ref[...], rec_prev_ref[...])

    def store_split(z_at, value):
        high, low = split_two(value)
        split_ref[pl.ds(z_at * full_y, full_y), 0:cols] = low
        split_ref[pl.ds(z_at * full_y, full_y), cols : 2 * cols] = high

    for z_at in range(full_z):
        store_split(z_at, field_a[HALO + z_at, y0 : y0 + full_y, :])

    def advance(tick, state, older):
        weights = jnp.concatenate([base_ref[2 * cols : 3 * cols], inject_ref[tick]], axis=0)
        for z_at in range(full_z):
            within = z_at % LAYERS
            if within == 0:
                part = pl.ds(z_at * full_y, min(LAYERS, full_z - z_at) * full_y)
                inline = jnp.dot(
                    split_ref[part, 0 : 2 * cols], base_ref[0 : 2 * cols], preferred_element_type=f32
                ) + jnp.dot(split_ref[part, cols : 3 * cols], weights, preferred_element_type=f32)
            total = inline[within * full_y : (within + 1) * full_y]
            z_in = HALO + z_at
            centre = state[z_in, y0 : y0 + full_y, :]
            for distance in range(1, 5):
                pairs = state[z_in - distance, y0 : y0 + full_y, :] + state[z_in + distance, y0 : y0 + full_y, :]
                pairs = pairs + (
                    state[z_in, y0 - distance : y0 - distance + full_y, :]
                    + state[z_in, y0 + distance : y0 + distance + full_y, :]
                )
                total = total + STENCIL_WEIGHTS[distance] * pairs
            updated = (2.0 * centre - older[z_in, y0 : y0 + full_y, :]) + speed_ref[z_at] * total
            older[z_in, y0 : y0 + full_y, :] = updated
            store_split(z_at, updated)

    partner_role = 2 * column + 1 - core
    deep = depth + 2

    def snap_copy(snapshot):
        return pltpu.make_async_remote_copy(
            src_ref=stage_ref.at[snapshot],
            dst_ref=snap_ref.at[snapshot, core],
            send_sem=snap_send.at[snapshot],
            recv_sem=snap_recv.at[snapshot],
            device_id=partner,
            device_id_type=MESH,
        )

    def one_image(snapshot, carry):
        @pl.when((snapshot == IMAGES // 2) & (core == 1))
        def _():
            for part in range(2):
                lend_copy(part).wait_recv()

        for pair in range(SUB // 2):
            advance(SUB * snapshot + 2 * pair, field_a, field_b)
            advance(SUB * snapshot + 2 * pair + 1, field_b, field_a)
        stage_ref[snapshot] = field_a[pl.ds(HALO - 1 + depth * partner_role, deep), own_y, :]
        snap_copy(snapshot).start()
        snap_ref[snapshot, core] = field_a[pl.ds(HALO - 1 + depth * role, deep), own_y, :]
        return carry

    lax.fori_loop(0, IMAGES, one_image, 0)
    for snapshot in range(IMAGES):
        snap_copy(snapshot).wait()
    results = [
        pltpu.make_async_copy(snap_ref.at[IMAGES - 1, side, pl.ds(1, depth)], kept, out_sem.at[side])
        for side, kept in enumerate((src_out_ref, rec_out_ref))
    ]
    for result in results:
        result.start()

    def one_lag(slot, carry):
        lag = lags_ref[slot]
        back = jnp.where(lag > 0, cols - 2 * lag, -2 * lag)
        shift = jnp.where(lag < 0, cols + lag, lag)
        summed = jnp.zeros((deep * rows, cols), f32)
        for snapshot in range(IMAGES):
            moved = pltpu.roll(snap_ref[snapshot, 1].reshape(deep * rows, cols), back, 1)
            summed = summed + snap_ref[snapshot, 0].reshape(deep * rows, cols) * moved
        filtered = (
            2.0 * summed[rows : rows + cells] - summed[0:cells] - summed[2 * rows : 2 * rows + cells]
        )
        filtered = pltpu.roll(filtered, shift, 1)
        lane = lax.broadcasted_iota(jnp.int32, (cells, cols), 1)
        reach = jnp.abs(lag)
        inside = (lane >= reach) & (lane < cols - reach)
        at = pl.multiple_of(slot * cells, cells)
        image_buf[pl.ds(at, cells)] = jnp.where(inside, filtered, 0.0).astype(jnp.bfloat16)
        return carry

    lag_count = lags_ref.shape[0]
    group = -(-lag_count // 4)
    for turn, start in enumerate(range(0, lag_count, group)):
        stop = min(start + group, lag_count)
        lax.fori_loop(start, stop, one_lag, 0, unroll=group)
        part = pl.ds(start * cells, (stop - start) * cells)
        result = pltpu.make_async_copy(image_buf.at[part], image_ref.at[part], out_sem.at[2 + turn])
        result.start()
        results.append(result)
    for result in results:
        result.wait()
    @pl.when(core == 0)
    def _():
        for part in range(2):
            lend_copy(part).wait_send()

    for copy in sends:
        copy.wait_send()


def hand_over(*refs):
    given, kept, held = refs[:3], refs[3:6], refs[6:9]
    first, last = refs[9:]
    arrive = [pltpu.make_async_copy(given[at], held[at], first.at[at]) for at in range(3)]
    leave = [pltpu.make_async_copy(held[at], kept[at], last.at[at]) for at in range(3)]
    for copy in arrive:
        copy.start()
    for at in (1, 2, 0):
        arrive[at].wait()
        leave[at].start()
    for copy in leave:
        copy.wait()


def window_shards(bands, roles, *arrays):
    rec_pos, rec_traces, offset_lags = arrays[8:]
    depth, rows, cols = arrays[0].shape
    cells = depth * rows
    full_z, full_y = depth * roles, rows * bands
    lag_count = offset_lags.shape[0]
    columns = roles // 2
    steps = SUB * IMAGES
    f32, bf16 = jnp.float32, jnp.bfloat16
    hbm = pl.BlockSpec(memory_space=pltpu.HBM)
    arrays = arrays[:8] + (rec_pos.T, rec_traces.T, offset_lags)
    places = [pltpu.SMEM if at in (1, 6, 7, 10) else pltpu.VMEM for at in range(len(arrays))]
    padded = (full_z + 2 * HALO, full_y + 16, cols)
    results = pl.pallas_call(
        functools.partial(window_kernel, bands, roles),
        out_shape=(
            jax.ShapeDtypeStruct((lag_count * cells, cols), bf16),
            jax.ShapeDtypeStruct((depth, rows, cols), f32),
            jax.ShapeDtypeStruct((depth, rows, cols), f32),
        ),
        in_specs=[hbm] * len(arrays),
        out_specs=(hbm, hbm, hbm),
        scratch_shapes=[place(array.shape, array.dtype) for place, array in zip(places, arrays)]
        + [
            pltpu.VMEM((2, 3 * cells, cols), WIRE),
            pltpu.VMEM((bands * roles, 3 * cells, cols), WIRE),
            pltpu.VMEM(padded, f32),
            pltpu.VMEM(padded, f32),
            pltpu.VMEM((full_z, full_y, cols), f32),
            pltpu.VMEM((full_z * full_y, 3 * cols), bf16),
            pltpu.VMEM((3 * cols, cols), bf16),
            pltpu.VMEM((steps, cols, cols), bf16),
            pltpu.VMEM((IMAGES, depth + 2, rows, cols), f32),
            pltpu.VMEM((IMAGES, 2, depth + 2, rows, cols), f32),
            pltpu.SemaphoreType.DMA((2 * bands,)),
            pltpu.SemaphoreType.DMA((2 * bands * columns,)),
            pltpu.SemaphoreType.DMA((bands * roles,)),
            pltpu.SemaphoreType.DMA((IMAGES,)),
            pltpu.SemaphoreType.DMA((IMAGES,)),
            pltpu.VMEM((2, steps // 2, full_y, cols), bf16),
            pltpu.VMEM((lag_count * cells, cols), bf16),
            pltpu.SemaphoreType.DMA((6,)),
            pltpu.SemaphoreType.DMA((len(arrays),)),
            pltpu.SemaphoreType.DMA((2,)),
            pltpu.SemaphoreType.DMA((2,)),
        ],
        compiler_params=pltpu.CompilerParams(
            collective_id=0, has_side_effects=True, vmem_limit_bytes=VMEM_GRANT
        ),
    )(*arrays)
    image, source, receiver = pl.pallas_call(
        hand_over,
        out_shape=tuple(jax.ShapeDtypeStruct(result.shape, result.dtype) for result in results),
        in_specs=[hbm] * 3,
        out_specs=(hbm, hbm, hbm),
        scratch_shapes=[pltpu.VMEM(result.shape, result.dtype) for result in results]
        + [pltpu.SemaphoreType.DMA((3,)), pltpu.SemaphoreType.DMA((3,))],
        compiler_params=pltpu.CompilerParams(vmem_limit_bytes=VMEM_GRANT),
    )(*results)
    return image.reshape(lag_count, depth, rows, cols), source, receiver


def shards(bands, roles, *arrays):
    depth, rows, cols = arrays[0].shape
    sources = arrays[6].shape[0]
    small = depth * roles * rows * bands * cols <= WINDOW_CELLS
    fits = roles % 2 == 0 and rows % 8 == 0 and cols % 128 == 0
    fits = fits and max(rows * bands, sources) <= cols // 2 and arrays[10].shape[0] < cols
    fits = fits and (depth * rows) % 16 == 0 and arrays[1].shape[0] <= 256
    if small and fits:
        return window_shards(bands, roles, *arrays)
    return tile_shards(*arrays)


def solution(mesh):
    placed = (
        P("role", "band", None),
        P(),
        P(("survey", "role"), "band", None),
        P(("survey", "role"), "band", None),
        P(("survey", "role"), "band", None),
        P(("survey", "role"), "band", None),
        P("survey", None),
        P("survey", None),
        P("survey", None),
        P("survey", None),
        P(),
    )
    return jax.shard_map(
        functools.partial(shards, mesh.shape["band"], mesh.shape["role"]),
        mesh=mesh,
        in_specs=placed,
        out_specs=(
            P("survey", "role", "band", None),
            P(("survey", "role"), "band", None),
            P(("survey", "role"), "band", None),
        ),
        check_vma=False,
    )
```

```python
import functools

import jax
import jax.numpy as jnp
from jax import lax
from jax.experimental import pallas as pl
from jax.experimental.pallas import tpu as pltpu
from jax.sharding import PartitionSpec as P

SUB = 4
IMAGES = 4
HALO = 4
WINDOW_CELLS = 1 << 17
MESH = pl.DeviceIdType.MESH
STRIP = 16
WIRE = jnp.bfloat16
VMEM_GRANT = 64 * 1024 * 1024


STENCIL_WEIGHTS = (-205.0 / 72.0, 8.0 / 5.0, -1.0 / 5.0, 8.0 / 315.0, -1.0 / 560.0)


def padded_2(block, sides, width):
    for axis, dim in sides:
        count = lax.axis_size(axis)
        forward = [(i, i + 1) for i in range(count - 1)]
        backward = [(target, source) for source, target in forward]
        low = lax.ppermute(
            lax.slice_in_dim(block, block.shape[dim] - width, None, axis=dim), axis, forward
        )
        high = lax.ppermute(lax.slice_in_dim(block, 0, width, axis=dim), axis, backward)
        block = jnp.concatenate([low, block, high], axis=dim)
    return block


def laplace(padded, depth_cells, row_cells, col_cells):

    def window(along_z, along_y, along_x):
        return padded[
            :,
            4 + along_z : 4 + along_z + depth_cells,
            4 + along_y : 4 + along_y + row_cells,
            4 + along_x : 4 + along_x + col_cells,
        ]

    summed = 3.0 * STENCIL_WEIGHTS[0] * window(0, 0, 0)
    for distance in range(1, 5):
        weight = STENCIL_WEIGHTS[distance]
        pairs = window(distance, 0, 0) + window(-distance, 0, 0)
        pairs = pairs + window(0, distance, 0) + window(0, -distance, 0)
        pairs = pairs + window(0, 0, distance) + window(0, 0, -distance)
        summed = summed + weight * pairs
    return summed


def lookup(vel_index, courant):
    levels = courant.shape[0]

    def add_level(level, summed):
        return summed + jnp.where(vel_index == level, courant[level], 0.0)

    return lax.fori_loop(0, levels, add_level, jnp.zeros(vel_index.shape, jnp.float32))


def local_index(global_at, start, extent):
    local_at = global_at - start
    inside = (local_at >= 0) & (local_at < extent)
    return jnp.where(inside, local_at, extent)


def inject_all(shape, depth_at, row_at, col_at, amounts):
    step_count = amounts.shape[1]
    return (
        jnp.zeros((step_count,) + shape, jnp.float32)
        .at[:, depth_at, row_at, col_at]
        .add(amounts.T, mode="drop")
    )


def lag_products(source_pad, receiver_pad, offset_lags, max_lag, col_cells):

    def product(lag_value):
        src_part = lax.dynamic_slice_in_dim(source_pad, max_lag - lag_value, col_cells, 2)
        rec_part = lax.dynamic_slice_in_dim(receiver_pad, max_lag + lag_value, col_cells, 2)
        return src_part * rec_part

    return jax.vmap(product)(offset_lags)


def depth_filter(padded, depth_cells):
    return (
        2.0 * padded[:, 1 : 1 + depth_cells]
        - padded[:, 0:depth_cells]
        - padded[:, 2 : 2 + depth_cells]
    )


def pad_inline(state, max_lag):
    return jnp.pad(state, ((0, 0), (0, 0), (0, 0), (max_lag, max_lag)))


def accumulate(slab_state, image_sum, edge_sum, offset_lags, max_lag):
    col_cells = slab_state.shape[3]
    padded = pad_inline(slab_state, max_lag)
    image_sum = image_sum + lag_products(padded[0], padded[1], offset_lags, max_lag, col_cells)
    return (image_sum, edge_sum)


def finish(image_sum):
    padded = padded_2(image_sum, (("role", 1),), 1)
    return depth_filter(padded, image_sum.shape[1]).astype(jnp.bfloat16)


def tile_shards(
    vel_index,
    courant,
    src_now,
    src_prev,
    rec_now,
    rec_prev,
    src_pos,
    src_wavelet,
    rec_pos,
    rec_traces,
    offset_lags,
):
    lag_count = offset_lags.shape[0]
    max_lag = lag_count // 2
    speed = lookup(vel_index, courant)
    band_start = lax.axis_index("band") * src_now.shape[1]
    role_at = lax.axis_index("role")
    current = jnp.stack([src_now, rec_now])
    previous = jnp.stack([src_prev, rec_prev])
    depth_start = role_at * src_now.shape[0]
    col_start = 0

    def faces(state):
        padded = padded_2(state, (("band", 2), ("role", 1)), 4)
        return jnp.pad(padded, ((0, 0), (0, 0), (0, 0), (4, 4)))

    depth_cells, row_cells, col_cells = speed.shape
    shape = speed.shape
    slab_shape = src_now.shape
    src_depth = local_index(src_pos[:, 0], depth_start, depth_cells)
    src_row = local_index(src_pos[:, 1], band_start, row_cells)
    src_col = local_index(src_pos[:, 2], col_start, col_cells)
    rec_depth = local_index(jnp.zeros_like(rec_pos[:, 0]), depth_start, depth_cells)
    rec_row = local_index(rec_pos[:, 0], band_start, row_cells)
    rec_col = local_index(rec_pos[:, 1], col_start, col_cells)
    src_terms = inject_all(shape, src_depth, src_row, src_col, src_wavelet)
    rec_terms = inject_all(shape, rec_depth, rec_row, rec_col, rec_traces)
    image_sum = jnp.zeros((lag_count,) + slab_shape, jnp.float32)
    edge_sum = jnp.zeros((lag_count, 2) + slab_shape[1:], jnp.float32)
    slab_state = current
    for snapshot in range(IMAGES):

        def advance(substep, carry):
            state, older = carry
            tick_at = snapshot * SUB + substep
            sources = jnp.stack(
                [
                    lax.dynamic_index_in_dim(src_terms, tick_at, 0, keepdims=False),
                    lax.dynamic_index_in_dim(rec_terms, tick_at, 0, keepdims=False),
                ]
            )
            laplacian = laplace(faces(state), depth_cells, row_cells, col_cells)
            updated = 2.0 * state - older + speed * (laplacian + sources)
            return (updated, state)

        current, previous = lax.fori_loop(0, SUB, advance, (current, previous))
        slab_state = current
        image_sum, edge_sum = accumulate(slab_state, image_sum, edge_sum, offset_lags, max_lag)
    image = finish(image_sum)
    return (image, slab_state[0], slab_state[1])


def split_two(value):
    high = value.astype(jnp.bfloat16)
    low = (value - high.astype(jnp.float32)).astype(jnp.bfloat16)
    return high, low


def inline_matrix(cols):
    row = lax.broadcasted_iota(jnp.int32, (cols, cols), 0)
    col = lax.broadcasted_iota(jnp.int32, (cols, cols), 1)
    apart = jnp.abs(row - col)
    matrix = jnp.where(apart == 0, 3.0 * STENCIL_WEIGHTS[0], 0.0)
    for distance in range(1, 5):
        matrix = jnp.where(apart == distance, STENCIL_WEIGHTS[distance], matrix)
    return matrix


def window_kernel(
    bands,
    roles,
    *refs,
):
    inputs, outputs, held = refs[:11], refs[11:14], refs[14:25]
    (
        vel_ref,
        courant_ref,
        src_now_ref,
        src_prev_ref,
        rec_now_ref,
        rec_prev_ref,
        src_pos_ref,
        src_wave_ref,
        rec_pos_ref,
        rec_trace_ref,
        lags_ref,
    ) = held
    image_ref, src_out_ref, rec_out_ref = outputs
    (
        out_buf,
        blocks,
        field_a,
        field_b,
        speed_ref,
        split_ref,
        base_ref,
        inject_ref,
        stage_ref,
        snap_ref,
        near_send,
        far_send,
        block_recv,
        snap_send,
        snap_recv,
        lend_ref,
        image_buf,
        early_ref,
        out_sem,
        in_sem,
        lend_send,
        lend_recv,
    ) = refs[25:]
    fetches = [
        pltpu.make_async_copy(given, kept, in_sem.at[at])
        for at, (given, kept) in enumerate(zip(inputs, held))
    ]
    for fetch in fetches:
        fetch.start()
    inject_ref[...] = jnp.zeros_like(inject_ref)
    depth, rows, cols = vel_ref.shape
    full_z, full_y = depth * roles, rows * bands
    cells = depth * rows
    columns = roles // 2
    survey = lax.axis_index("survey")
    band = lax.axis_index("band")
    role = lax.axis_index("role")
    core = lax.rem(role, 2)
    column = role // 2
    own = band * roles + role
    f32 = jnp.float32
    y0 = 8

    def device(at_band, at_role):
        return (survey, at_band, at_role)

    partner = device(band, 2 * column + 1 - core)
    barrier = pltpu.get_barrier_semaphore()
    greeted = 0
    for step in range(1, bands):
        for side in range(2):
            pl.semaphore_signal(
                barrier,
                inc=1,
                device_id=device(lax.rem(band + step, bands), 2 * column + side),
                device_id_type=MESH,
            )
            greeted += 1
    pl.semaphore_signal(barrier, inc=1, device_id=partner, device_id_type=MESH)
    greeted += 1
    for step in range(1, columns):
        pl.semaphore_signal(
            barrier,
            inc=1,
            device_id=device(band, 2 * lax.rem(column + step, columns) + core),
            device_id_type=MESH,
        )
        greeted += 1

    for at in (0, 2, 3, 4, 5):
        fetches[at].wait()
    index = vel_ref[...].astype(f32).reshape(cells, cols)
    for side, now_ref, prev_ref in ((0, src_now_ref, src_prev_ref), (1, rec_now_ref, rec_prev_ref)):
        now = now_ref[...].reshape(cells, cols)
        change = now - prev_ref[...].reshape(cells, cols)
        out_buf[side, 0:cells] = now.astype(WIRE)
        out_buf[side, cells : 2 * cells] = change.astype(WIRE)
        out_buf[side, 2 * cells : 3 * cells] = index.astype(WIRE)
    pl.semaphore_wait(barrier, greeted)

    sends = []
    for step in range(1, bands):
        for side in range(2):
            copy = pltpu.make_async_remote_copy(
                src_ref=out_buf.at[side],
                dst_ref=blocks.at[own],
                send_sem=near_send.at[2 * step + side],
                recv_sem=block_recv.at[own],
                device_id=device(lax.rem(band + step, bands), 2 * column + side),
                device_id_type=MESH,
            )
            copy.start()
            sends.append(copy)
    copy = pltpu.make_async_remote_copy(
        src_ref=out_buf.at[1 - core],
        dst_ref=blocks.at[own],
        send_sem=near_send.at[0],
        recv_sem=block_recv.at[own],
        device_id=partner,
        device_id_type=MESH,
    )
    copy.start()
    sends.append(copy)

    def pass_on(step, source, slot, lane):
        copy = pltpu.make_async_remote_copy(
            src_ref=source,
            dst_ref=blocks.at[slot],
            send_sem=far_send.at[lane],
            recv_sem=block_recv.at[slot],
            device_id=device(band, 2 * lax.rem(column + step, columns) + core),
            device_id_type=MESH,
        )
        copy.start()
        sends.append(copy)

    def landed(slot):
        pltpu.make_async_copy(blocks.at[slot], blocks.at[slot], block_recv.at[slot]).wait()

    for step in range(1, columns):
        pass_on(step, out_buf.at[core], own, step)

    for at in (1, 6, 7, 8, 9, 10):
        fetches[at].wait()
    lines = split_ref.shape[0]
    half = cols // 2
    row_at = lax.broadcasted_iota(jnp.int32, (lines, cols), 0)
    lane_at = lax.broadcasted_iota(jnp.int32, (lines, cols), 1)
    lane_low = jnp.where(lane_at >= half, lane_at - half, lane_at)
    steps = inject_ref.shape[0]

    @pl.when(core == 0)
    def _():
        count = src_pos_ref.shape[0]
        target = jnp.full((1, cols), -1, jnp.int32)
        lane = lax.broadcasted_iota(jnp.int32, (1, cols), 1)
        lane = jnp.where(lane >= half, lane - half, lane)
        for source in range(count):
            y_at = src_pos_ref[source, 1]
            strip = lax.div(y_at, STRIP)
            line = (strip * full_z + src_pos_ref[source, 0]) * STRIP + y_at - strip * STRIP
            target = jnp.where(lane == source, line, target)
        split_ref[:, 2 * cols : 3 * cols] = jnp.where(row_at == target, 1.0, 0.0).astype(jnp.bfloat16)
        height = -(-count // 16) * 16
        row = lax.broadcasted_iota(jnp.int32, (height, cols), 0)
        col = lax.broadcasted_iota(jnp.int32, (height, cols), 1)
        for tick in range(steps):
            term = jnp.zeros((height, cols), f32)
            for source in range(count):
                here = (row == source) & (col == src_pos_ref[source, 2])
                term = jnp.where(here, src_wave_ref[source, tick], term)
            high, low = split_two(term)
            inject_ref[tick, 0:height] = high
            inject_ref[tick, half : half + height] = low

    high, low = split_two(inline_matrix(cols))
    base_ref[0:cols] = high
    base_ref[cols : 2 * cols] = high
    base_ref[2 * cols : 3 * cols] = low
    field_a[...] = jnp.zeros_like(field_a)
    field_b[...] = jnp.zeros_like(field_b)

    @pl.when(core == 1)
    def _():
        split_ref[:, 2 * cols : 3 * cols] = jnp.zeros((lines, cols), jnp.bfloat16)
        for strip in range(full_y // STRIP):
            same = row_at[0:STRIP] + strip * STRIP == lane_low[0:STRIP]
            top = pl.ds(strip * full_z * STRIP, STRIP)
            split_ref[top, 2 * cols : 3 * cols] = jnp.where(same, 1.0, 0.0).astype(jnp.bfloat16)

    share = steps // 2
    first = pl.multiple_of(share * (1 - core), share)
    count = rec_pos_ref.shape[1]
    chunk = min(512, count)

    def add_receivers(total, start, stop):
        for at in range(start, stop, chunk):
            size = min(chunk, stop - at)
            y_at = rec_pos_ref[0:1, at : at + size]
            x_at = rec_pos_ref[1:2, at : at + size]
            in_row = lax.broadcasted_iota(jnp.int32, (full_y, size), 0) == y_at
            in_col = lax.broadcasted_iota(jnp.int32, (cols, size), 0) == x_at
            in_col = jnp.where(in_col, 1.0, 0.0).astype(jnp.bfloat16)
            amounts = rec_trace_ref[pl.ds(first, share), at : at + size]
            high = amounts.astype(jnp.bfloat16).astype(f32)
            parts = []
            for part in (high, amounts - high):
                for tick in range(share):
                    parts.append(jnp.where(in_row, part[tick : tick + 1], 0.0).astype(jnp.bfloat16))
            total = total + lax.dot_general(
                jnp.concatenate(parts, axis=0),
                in_col,
                (((1,), (1,)), ((), ())),
                preferred_element_type=f32,
            )
        return total

    middle = count // 2 // chunk * chunk
    added = add_receivers(jnp.zeros((2 * share * full_y, cols), f32), 0, middle)

    slot = band * roles + 2 * column + 1 - core
    landed(slot)
    for step in range(1, columns):
        pass_on(step, blocks.at[slot], slot, columns + step)
    for hop in range(1, bands):
        for side in range(2):
            slot = lax.rem(band + hop, bands) * roles + 2 * column + side
            landed(slot)
            for step in range(1, columns):
                pass_on(step, blocks.at[slot], slot, (2 * hop + side) * columns + step)
    added = add_receivers(added, middle, count)
    size = share * full_y
    high, low = split_two(added[0:size] + added[size : 2 * size])
    lend_ref[0] = high.reshape(share, full_y, cols)
    lend_ref[1] = low.reshape(share, full_y, cols)

    def lend_copy(part):
        return pltpu.make_async_remote_copy(
            src_ref=lend_ref.at[part],
            dst_ref=inject_ref.at[pl.ds(share, share), pl.ds(part * half, full_y)],
            send_sem=lend_send.at[part],
            recv_sem=lend_recv.at[part],
            device_id=partner,
            device_id_type=MESH,
        )

    @pl.when(core == 0)
    def _():
        for part in range(2):
            lend_copy(part).start()

    @pl.when(core == 1)
    def _():
        for part in range(2):
            inject_ref[0:share, part * half : part * half + full_y] = lend_ref[part]

    def table(values):
        found = jnp.zeros(values.shape, f32)
        for level in range(courant_ref.shape[0]):
            found = jnp.where(values == float(level), courant_ref[level], found)
        return found

    def unpack(at_band, at_role, block):
        now = block[0:cells].reshape(depth, rows, cols)
        prev = now - block[cells : 2 * cells].reshape(depth, rows, cols)
        z_part = pl.ds(HALO + depth * at_role, depth)
        y_part = pl.ds(pl.multiple_of(y0 + rows * at_band, rows), rows)
        field_a[z_part, y_part, :] = now
        field_b[z_part, y_part, :] = prev
        speed_ref[pl.ds(depth * at_role, depth), pl.ds(pl.multiple_of(rows * at_band, rows), rows), :] = table(
            block[2 * cells : 3 * cells]
        ).reshape(depth, rows, cols)

    for hop in range(bands):
        for side in range(2):
            at_band, at_role = lax.rem(band + hop, bands), 2 * column + lax.rem(core + side, 2)
            if hop == 0 and side == 0:
                unpack(band, role, out_buf[core].astype(f32))
            else:
                unpack(at_band, at_role, blocks[at_band * roles + at_role].astype(f32))
    for hop in range(bands):
        for step in range(1, columns):
            for side in range(2):
                at_band = lax.rem(band + hop, bands)
                at_role = 2 * lax.rem(column + step, columns) + lax.rem(core + side, 2)
                landed(at_band * roles + at_role)
                unpack(at_band, at_role, blocks[at_band * roles + at_role].astype(f32))

    own_z = pl.ds(HALO + depth * role, depth)
    own_y = pl.ds(pl.multiple_of(y0 + rows * band, rows), rows)
    field_a[own_z, own_y, :] = jnp.where(core == 0, src_now_ref[...], rec_now_ref[...])
    field_b[own_z, own_y, :] = jnp.where(core == 0, src_prev_ref[...], rec_prev_ref[...])

    def store_split(strip, z_at, value):
        high, low = split_two(value)
        line = pl.ds((strip * full_z + z_at) * STRIP, STRIP)
        split_ref[line, 0:cols] = low
        split_ref[line, cols : 2 * cols] = high

    for strip in range(full_y // STRIP):
        for z_at in range(full_z):
            at = y0 + strip * STRIP
            store_split(strip, z_at, field_a[HALO + z_at, at : at + STRIP, :])

    def advance(tick, state, older):
        weights = jnp.concatenate([base_ref[2 * cols : 3 * cols], inject_ref[tick]], axis=0)
        for strip in range(full_y // STRIP):
            at = y0 + strip * STRIP
            part = pl.ds(strip * full_z * STRIP, full_z * STRIP)
            inline = jnp.dot(
                split_ref[part, 0 : 2 * cols], base_ref[0 : 2 * cols], preferred_element_type=f32
            ) + jnp.dot(split_ref[part, cols : 3 * cols], weights, preferred_element_type=f32)
            layers = [state[HALO + z_at, at : at + STRIP, :] for z_at in range(full_z)]
            for z_at in range(full_z):
                total = inline[z_at * STRIP : (z_at + 1) * STRIP]
                z_in = HALO + z_at
                for distance in range(1, 5):
                    pairs = (
                        state[z_in, at - distance : at - distance + STRIP, :]
                        + state[z_in, at + distance : at + distance + STRIP, :]
                    )
                    for other in (z_at - distance, z_at + distance):
                        if 0 <= other < full_z:
                            pairs = pairs + layers[other]
                    total = total + STENCIL_WEIGHTS[distance] * pairs
                updated = (2.0 * layers[z_at] - older[z_in, at : at + STRIP, :]) + (
                    speed_ref[z_at, strip * STRIP : (strip + 1) * STRIP] * total
                )
                older[z_in, at : at + STRIP, :] = updated
                store_split(strip, z_at, updated)

    partner_role = 2 * column + 1 - core
    deep = depth + 2

    def snap_copy(snapshot):
        return pltpu.make_async_remote_copy(
            src_ref=stage_ref.at[snapshot],
            dst_ref=snap_ref.at[snapshot, core],
            send_sem=snap_send.at[snapshot],
            recv_sem=snap_recv.at[snapshot],
            device_id=partner,
            device_id_type=MESH,
        )

    def one_image(snapshot, carry):
        @pl.when((snapshot == IMAGES // 2) & (core == 1))
        def _():
            for part in range(2):
                lend_copy(part).wait_recv()

        for pair in range(SUB // 2):
            advance(SUB * snapshot + 2 * pair, field_a, field_b)
            advance(SUB * snapshot + 2 * pair + 1, field_b, field_a)
        stage_ref[snapshot] = field_a[pl.ds(HALO - 1 + depth * partner_role, deep), own_y, :]
        snap_copy(snapshot).start()
        snap_ref[snapshot, core] = field_a[pl.ds(HALO - 1 + depth * role, deep), own_y, :]
        return carry

    lax.fori_loop(0, IMAGES, one_image, 0)
    def correlate(slot, snapshots, summed):
        lag = lags_ref[slot]
        back = jnp.where(lag > 0, cols - 2 * lag, -2 * lag)
        for snapshot in snapshots:
            moved = pltpu.roll(snap_ref[snapshot, 1].reshape(deep * rows, cols), back, 1)
            summed = summed + snap_ref[snapshot, 0].reshape(deep * rows, cols) * moved
        return summed

    lag_count = lags_ref.shape[0]
    group = -(-lag_count // 4)
    last = IMAGES - 1
    for snapshot in range(last):
        snap_copy(snapshot).wait()

    def early_lag(slot, carry):
        early_ref[slot] = correlate(slot, range(last), jnp.zeros((deep * rows, cols), f32))
        return carry

    lax.fori_loop(0, lag_count, early_lag, 0, unroll=group)
    snap_copy(last).wait()
    results = [
        pltpu.make_async_copy(snap_ref.at[IMAGES - 1, side, pl.ds(1, depth)], kept, out_sem.at[side])
        for side, kept in enumerate((src_out_ref, rec_out_ref))
    ]
    for result in results:
        result.start()

    def one_lag(slot, carry):
        lag = lags_ref[slot]
        shift = jnp.where(lag < 0, cols + lag, lag)
        summed = correlate(slot, (last,), early_ref[slot])
        filtered = (
            2.0 * summed[rows : rows + cells] - summed[0:cells] - summed[2 * rows : 2 * rows + cells]
        )
        filtered = pltpu.roll(filtered, shift, 1)
        lane = lax.broadcasted_iota(jnp.int32, (cells, cols), 1)
        reach = jnp.abs(lag)
        inside = (lane >= reach) & (lane < cols - reach)
        at = pl.multiple_of(slot * cells, cells)
        image_buf[pl.ds(at, cells)] = jnp.where(inside, filtered, 0.0).astype(jnp.bfloat16)
        return carry

    for turn, start in enumerate(range(0, lag_count, group)):
        stop = min(start + group, lag_count)
        lax.fori_loop(start, stop, one_lag, 0, unroll=group)
        part = pl.ds(start * cells, (stop - start) * cells)
        result = pltpu.make_async_copy(image_buf.at[part], image_ref.at[part], out_sem.at[2 + turn])
        result.start()
        results.append(result)
    for result in results:
        result.wait()
    @pl.when(core == 0)
    def _():
        for part in range(2):
            lend_copy(part).wait_send()

    for copy in sends:
        copy.wait_send()


def hand_over(*refs):
    given, kept, held = refs[:3], refs[3:6], refs[6:9]
    first, last = refs[9:]
    arrive = [pltpu.make_async_copy(given[at], held[at], first.at[at]) for at in range(3)]
    leave = [pltpu.make_async_copy(held[at], kept[at], last.at[at]) for at in range(3)]
    for copy in arrive:
        copy.start()
    for at in (1, 2, 0):
        arrive[at].wait()
        leave[at].start()
    for copy in leave:
        copy.wait()


def window_shards(bands, roles, *arrays):
    rec_pos, rec_traces, offset_lags = arrays[8:]
    depth, rows, cols = arrays[0].shape
    cells = depth * rows
    full_z, full_y = depth * roles, rows * bands
    lag_count = offset_lags.shape[0]
    columns = roles // 2
    steps = SUB * IMAGES
    f32, bf16 = jnp.float32, jnp.bfloat16
    hbm = pl.BlockSpec(memory_space=pltpu.HBM)
    arrays = arrays[:8] + (rec_pos.T, rec_traces.T, offset_lags)
    places = [pltpu.SMEM if at in (1, 6, 7, 10) else pltpu.VMEM for at in range(len(arrays))]
    padded = (full_z + 2 * HALO, full_y + 16, cols)
    results = pl.pallas_call(
        functools.partial(window_kernel, bands, roles),
        out_shape=(
            jax.ShapeDtypeStruct((lag_count * cells, cols), bf16),
            jax.ShapeDtypeStruct((depth, rows, cols), f32),
            jax.ShapeDtypeStruct((depth, rows, cols), f32),
        ),
        in_specs=[hbm] * len(arrays),
        out_specs=(hbm, hbm, hbm),
        scratch_shapes=[place(array.shape, array.dtype) for place, array in zip(places, arrays)]
        + [
            pltpu.VMEM((2, 3 * cells, cols), WIRE),
            pltpu.VMEM((bands * roles, 3 * cells, cols), WIRE),
            pltpu.VMEM(padded, f32),
            pltpu.VMEM(padded, f32),
            pltpu.VMEM((full_z, full_y, cols), f32),
            pltpu.VMEM((full_z * full_y, 3 * cols), bf16),
            pltpu.VMEM((3 * cols, cols), bf16),
            pltpu.VMEM((steps, cols, cols), bf16),
            pltpu.VMEM((IMAGES, depth + 2, rows, cols), f32),
            pltpu.VMEM((IMAGES, 2, depth + 2, rows, cols), f32),
            pltpu.SemaphoreType.DMA((2 * bands,)),
            pltpu.SemaphoreType.DMA((2 * bands * columns,)),
            pltpu.SemaphoreType.DMA((bands * roles,)),
            pltpu.SemaphoreType.DMA((IMAGES,)),
            pltpu.SemaphoreType.DMA((IMAGES,)),
            pltpu.VMEM((2, steps // 2, full_y, cols), bf16),
            pltpu.VMEM((lag_count * cells, cols), bf16),
            pltpu.VMEM((lag_count, cells + 2 * rows, cols), f32),
            pltpu.SemaphoreType.DMA((6,)),
            pltpu.SemaphoreType.DMA((len(arrays),)),
            pltpu.SemaphoreType.DMA((2,)),
            pltpu.SemaphoreType.DMA((2,)),
        ],
        compiler_params=pltpu.CompilerParams(
            collective_id=0, has_side_effects=True, vmem_limit_bytes=VMEM_GRANT
        ),
    )(*arrays)
    image, source, receiver = pl.pallas_call(
        hand_over,
        out_shape=tuple(jax.ShapeDtypeStruct(result.shape, result.dtype) for result in results),
        in_specs=[hbm] * 3,
        out_specs=(hbm, hbm, hbm),
        scratch_shapes=[pltpu.VMEM(result.shape, result.dtype) for result in results]
        + [pltpu.SemaphoreType.DMA((3,)), pltpu.SemaphoreType.DMA((3,))],
        compiler_params=pltpu.CompilerParams(vmem_limit_bytes=VMEM_GRANT),
    )(*results)
    return image.reshape(lag_count, depth, rows, cols), source, receiver


def shards(bands, roles, *arrays):
    depth, rows, cols = arrays[0].shape
    sources = arrays[6].shape[0]
    small = depth * roles * rows * bands * cols <= WINDOW_CELLS
    fits = roles % 2 == 0 and rows % 8 == 0 and cols % 128 == 0
    fits = fits and max(rows * bands, sources) <= cols // 2 and arrays[10].shape[0] < cols
    fits = fits and (depth * rows) % 16 == 0 and (rows * bands) % STRIP == 0 and arrays[1].shape[0] <= 256
    if small and fits:
        return window_shards(bands, roles, *arrays)
    return tile_shards(*arrays)


def solution(mesh):
    placed = (
        P("role", "band", None),
        P(),
        P(("survey", "role"), "band", None),
        P(("survey", "role"), "band", None),
        P(("survey", "role"), "band", None),
        P(("survey", "role"), "band", None),
        P("survey", None),
        P("survey", None),
        P("survey", None),
        P("survey", None),
        P(),
    )
    return jax.shard_map(
        functools.partial(shards, mesh.shape["band"], mesh.shape["role"]),
        mesh=mesh,
        in_specs=placed,
        out_specs=(
            P("survey", "role", "band", None),
            P(("survey", "role"), "band", None),
            P(("survey", "role"), "band", None),
        ),
        check_vma=False,
    )
```

```python
import functools

import jax
import jax.numpy as jnp
from jax import lax
from jax.experimental import pallas as pl
from jax.experimental.pallas import tpu as pltpu
from jax.sharding import PartitionSpec as P

SUB = 4
IMAGES = 4
HALO = 4
WINDOW_CELLS = 1 << 17
MESH = pl.DeviceIdType.MESH
STRIP = 16
WIRE = jnp.bfloat16
VMEM_GRANT = 64 * 1024 * 1024


STENCIL_WEIGHTS = (-205.0 / 72.0, 8.0 / 5.0, -1.0 / 5.0, 8.0 / 315.0, -1.0 / 560.0)


def padded_2(block, sides, width):
    for axis, dim in sides:
        count = lax.axis_size(axis)
        forward = [(i, i + 1) for i in range(count - 1)]
        backward = [(target, source) for source, target in forward]
        low = lax.ppermute(
            lax.slice_in_dim(block, block.shape[dim] - width, None, axis=dim), axis, forward
        )
        high = lax.ppermute(lax.slice_in_dim(block, 0, width, axis=dim), axis, backward)
        block = jnp.concatenate([low, block, high], axis=dim)
    return block


def laplace(padded, depth_cells, row_cells, col_cells):

    def window(along_z, along_y, along_x):
        return padded[
            :,
            4 + along_z : 4 + along_z + depth_cells,
            4 + along_y : 4 + along_y + row_cells,
            4 + along_x : 4 + along_x + col_cells,
        ]

    summed = 3.0 * STENCIL_WEIGHTS[0] * window(0, 0, 0)
    for distance in range(1, 5):
        weight = STENCIL_WEIGHTS[distance]
        pairs = window(distance, 0, 0) + window(-distance, 0, 0)
        pairs = pairs + window(0, distance, 0) + window(0, -distance, 0)
        pairs = pairs + window(0, 0, distance) + window(0, 0, -distance)
        summed = summed + weight * pairs
    return summed


def lookup(vel_index, courant):
    levels = courant.shape[0]

    def add_level(level, summed):
        return summed + jnp.where(vel_index == level, courant[level], 0.0)

    return lax.fori_loop(0, levels, add_level, jnp.zeros(vel_index.shape, jnp.float32))


def local_index(global_at, start, extent):
    local_at = global_at - start
    inside = (local_at >= 0) & (local_at < extent)
    return jnp.where(inside, local_at, extent)


def inject_all(shape, depth_at, row_at, col_at, amounts):
    step_count = amounts.shape[1]
    return (
        jnp.zeros((step_count,) + shape, jnp.float32)
        .at[:, depth_at, row_at, col_at]
        .add(amounts.T, mode="drop")
    )


def lag_products(source_pad, receiver_pad, offset_lags, max_lag, col_cells):

    def product(lag_value):
        src_part = lax.dynamic_slice_in_dim(source_pad, max_lag - lag_value, col_cells, 2)
        rec_part = lax.dynamic_slice_in_dim(receiver_pad, max_lag + lag_value, col_cells, 2)
        return src_part * rec_part

    return jax.vmap(product)(offset_lags)


def depth_filter(padded, depth_cells):
    return (
        2.0 * padded[:, 1 : 1 + depth_cells]
        - padded[:, 0:depth_cells]
        - padded[:, 2 : 2 + depth_cells]
    )


def pad_inline(state, max_lag):
    return jnp.pad(state, ((0, 0), (0, 0), (0, 0), (max_lag, max_lag)))


def accumulate(slab_state, image_sum, edge_sum, offset_lags, max_lag):
    col_cells = slab_state.shape[3]
    padded = pad_inline(slab_state, max_lag)
    image_sum = image_sum + lag_products(padded[0], padded[1], offset_lags, max_lag, col_cells)
    return (image_sum, edge_sum)


def finish(image_sum):
    padded = padded_2(image_sum, (("role", 1),), 1)
    return depth_filter(padded, image_sum.shape[1]).astype(jnp.bfloat16)


def tile_shards(
    vel_index,
    courant,
    src_now,
    src_prev,
    rec_now,
    rec_prev,
    src_pos,
    src_wavelet,
    rec_pos,
    rec_traces,
    offset_lags,
):
    lag_count = offset_lags.shape[0]
    max_lag = lag_count // 2
    speed = lookup(vel_index, courant)
    band_start = lax.axis_index("band") * src_now.shape[1]
    role_at = lax.axis_index("role")
    current = jnp.stack([src_now, rec_now])
    previous = jnp.stack([src_prev, rec_prev])
    depth_start = role_at * src_now.shape[0]
    col_start = 0

    def faces(state):
        padded = padded_2(state, (("band", 2), ("role", 1)), 4)
        return jnp.pad(padded, ((0, 0), (0, 0), (0, 0), (4, 4)))

    depth_cells, row_cells, col_cells = speed.shape
    shape = speed.shape
    slab_shape = src_now.shape
    src_depth = local_index(src_pos[:, 0], depth_start, depth_cells)
    src_row = local_index(src_pos[:, 1], band_start, row_cells)
    src_col = local_index(src_pos[:, 2], col_start, col_cells)
    rec_depth = local_index(jnp.zeros_like(rec_pos[:, 0]), depth_start, depth_cells)
    rec_row = local_index(rec_pos[:, 0], band_start, row_cells)
    rec_col = local_index(rec_pos[:, 1], col_start, col_cells)
    src_terms = inject_all(shape, src_depth, src_row, src_col, src_wavelet)
    rec_terms = inject_all(shape, rec_depth, rec_row, rec_col, rec_traces)
    image_sum = jnp.zeros((lag_count,) + slab_shape, jnp.float32)
    edge_sum = jnp.zeros((lag_count, 2) + slab_shape[1:], jnp.float32)
    slab_state = current
    for snapshot in range(IMAGES):

        def advance(substep, carry):
            state, older = carry
            tick_at = snapshot * SUB + substep
            sources = jnp.stack(
                [
                    lax.dynamic_index_in_dim(src_terms, tick_at, 0, keepdims=False),
                    lax.dynamic_index_in_dim(rec_terms, tick_at, 0, keepdims=False),
                ]
            )
            laplacian = laplace(faces(state), depth_cells, row_cells, col_cells)
            updated = 2.0 * state - older + speed * (laplacian + sources)
            return (updated, state)

        current, previous = lax.fori_loop(0, SUB, advance, (current, previous))
        slab_state = current
        image_sum, edge_sum = accumulate(slab_state, image_sum, edge_sum, offset_lags, max_lag)
    image = finish(image_sum)
    return (image, slab_state[0], slab_state[1])


def split_two(value):
    high = value.astype(jnp.bfloat16)
    low = (value - high.astype(jnp.float32)).astype(jnp.bfloat16)
    return high, low


def inline_matrix(cols):
    row = lax.broadcasted_iota(jnp.int32, (cols, cols), 0)
    col = lax.broadcasted_iota(jnp.int32, (cols, cols), 1)
    apart = jnp.abs(row - col)
    matrix = jnp.where(apart == 0, 3.0 * STENCIL_WEIGHTS[0], 0.0)
    for distance in range(1, 5):
        matrix = jnp.where(apart == distance, STENCIL_WEIGHTS[distance], matrix)
    return matrix


def window_kernel(
    bands,
    roles,
    *refs,
):
    inputs, outputs, held = refs[:11], refs[11:14], refs[14:25]
    (
        vel_ref,
        courant_ref,
        src_now_ref,
        src_prev_ref,
        rec_now_ref,
        rec_prev_ref,
        src_pos_ref,
        src_wave_ref,
        rec_pos_ref,
        rec_trace_ref,
        lags_ref,
    ) = held
    image_ref, src_out_ref, rec_out_ref = outputs
    (
        out_buf,
        blocks,
        field_a,
        field_b,
        speed_ref,
        split_ref,
        base_ref,
        inject_ref,
        stage_ref,
        snap_ref,
        near_send,
        far_send,
        block_recv,
        snap_send,
        snap_recv,
        lend_ref,
        image_buf,
        early_ref,
        out_sem,
        in_sem,
        lend_send,
        lend_recv,
    ) = refs[25:]
    fetches = [
        pltpu.make_async_copy(given, kept, in_sem.at[at])
        for at, (given, kept) in enumerate(zip(inputs, held))
    ]
    for fetch in fetches:
        fetch.start()
    inject_ref[...] = jnp.zeros_like(inject_ref)
    depth, rows, cols = vel_ref.shape
    full_z, full_y = depth * roles, rows * bands
    cells = depth * rows
    columns = roles // 2
    survey = lax.axis_index("survey")
    band = lax.axis_index("band")
    role = lax.axis_index("role")
    core = lax.rem(role, 2)
    column = role // 2
    own = band * roles + role
    f32 = jnp.float32
    y0 = 8

    def device(at_band, at_role):
        return (survey, at_band, at_role)

    partner = device(band, 2 * column + 1 - core)
    barrier = pltpu.get_barrier_semaphore()
    greeted = 0
    for step in range(1, bands):
        for side in range(2):
            pl.semaphore_signal(
                barrier,
                inc=1,
                device_id=device(lax.rem(band + step, bands), 2 * column + side),
                device_id_type=MESH,
            )
            greeted += 1
    pl.semaphore_signal(barrier, inc=1, device_id=partner, device_id_type=MESH)
    greeted += 1
    for step in range(1, columns):
        pl.semaphore_signal(
            barrier,
            inc=1,
            device_id=device(band, 2 * lax.rem(column + step, columns) + core),
            device_id_type=MESH,
        )
        greeted += 1

    for at in (0, 2, 3, 4, 5):
        fetches[at].wait()
    index = vel_ref[...].astype(f32).reshape(cells, cols)
    for side, now_ref, prev_ref in ((0, src_now_ref, src_prev_ref), (1, rec_now_ref, rec_prev_ref)):
        now = now_ref[...].reshape(cells, cols)
        change = now - prev_ref[...].reshape(cells, cols)
        out_buf[side, 0:cells] = now.astype(WIRE)
        out_buf[side, cells : 2 * cells] = change.astype(WIRE)
        out_buf[side, 2 * cells : 3 * cells] = index.astype(WIRE)
    pl.semaphore_wait(barrier, greeted)

    sends = []
    for step in range(1, bands):
        for side in range(2):
            copy = pltpu.make_async_remote_copy(
                src_ref=out_buf.at[side],
                dst_ref=blocks.at[own],
                send_sem=near_send.at[2 * step + side],
                recv_sem=block_recv.at[own],
                device_id=device(lax.rem(band + step, bands), 2 * column + side),
                device_id_type=MESH,
            )
            copy.start()
            sends.append(copy)
    copy = pltpu.make_async_remote_copy(
        src_ref=out_buf.at[1 - core],
        dst_ref=blocks.at[own],
        send_sem=near_send.at[0],
        recv_sem=block_recv.at[own],
        device_id=partner,
        device_id_type=MESH,
    )
    copy.start()
    sends.append(copy)

    def pass_on(step, source, slot, lane):
        copy = pltpu.make_async_remote_copy(
            src_ref=source,
            dst_ref=blocks.at[slot],
            send_sem=far_send.at[lane],
            recv_sem=block_recv.at[slot],
            device_id=device(band, 2 * lax.rem(column + step, columns) + core),
            device_id_type=MESH,
        )
        copy.start()
        sends.append(copy)

    def landed(slot):
        pltpu.make_async_copy(blocks.at[slot], blocks.at[slot], block_recv.at[slot]).wait()

    for step in range(1, columns):
        pass_on(step, out_buf.at[core], own, step)

    high, low = split_two(inline_matrix(cols))
    base_ref[0:cols] = high
    base_ref[cols : 2 * cols] = high
    base_ref[2 * cols : 3 * cols] = low
    field_a[...] = jnp.zeros_like(field_a)
    field_b[...] = jnp.zeros_like(field_b)

    slot = band * roles + 2 * column + 1 - core
    landed(slot)
    for step in range(1, columns):
        pass_on(step, blocks.at[slot], slot, columns + step)

    for at in (1, 6, 7, 8, 9, 10):
        fetches[at].wait()
    lines = split_ref.shape[0]
    half = cols // 2
    row_at = lax.broadcasted_iota(jnp.int32, (lines, cols), 0)
    lane_at = lax.broadcasted_iota(jnp.int32, (lines, cols), 1)
    lane_low = jnp.where(lane_at >= half, lane_at - half, lane_at)
    steps = inject_ref.shape[0]

    @pl.when(core == 0)
    def _():
        count = src_pos_ref.shape[0]
        target = jnp.full((1, cols), -1, jnp.int32)
        lane = lax.broadcasted_iota(jnp.int32, (1, cols), 1)
        lane = jnp.where(lane >= half, lane - half, lane)
        for source in range(count):
            y_at = src_pos_ref[source, 1]
            strip = lax.div(y_at, STRIP)
            line = (strip * full_z + src_pos_ref[source, 0]) * STRIP + y_at - strip * STRIP
            target = jnp.where(lane == source, line, target)
        split_ref[:, 2 * cols : 3 * cols] = jnp.where(row_at == target, 1.0, 0.0).astype(jnp.bfloat16)
        height = -(-count // 16) * 16
        row = lax.broadcasted_iota(jnp.int32, (height, cols), 0)
        col = lax.broadcasted_iota(jnp.int32, (height, cols), 1)
        for tick in range(steps):
            term = jnp.zeros((height, cols), f32)
            for source in range(count):
                here = (row == source) & (col == src_pos_ref[source, 2])
                term = jnp.where(here, src_wave_ref[source, tick], term)
            high, low = split_two(term)
            inject_ref[tick, 0:height] = high
            inject_ref[tick, half : half + height] = low

    @pl.when(core == 1)
    def _():
        split_ref[:, 2 * cols : 3 * cols] = jnp.zeros((lines, cols), jnp.bfloat16)
        for strip in range(full_y // STRIP):
            same = row_at[0:STRIP] + strip * STRIP == lane_low[0:STRIP]
            top = pl.ds(strip * full_z * STRIP, STRIP)
            split_ref[top, 2 * cols : 3 * cols] = jnp.where(same, 1.0, 0.0).astype(jnp.bfloat16)

    share = steps // 2
    first = pl.multiple_of(share * (1 - core), share)
    count = rec_pos_ref.shape[1]
    chunk = min(512, count)

    def add_receivers(total, start, stop):
        for at in range(start, stop, chunk):
            size = min(chunk, stop - at)
            y_at = rec_pos_ref[0:1, at : at + size]
            x_at = rec_pos_ref[1:2, at : at + size]
            in_row = lax.broadcasted_iota(jnp.int32, (full_y, size), 0) == y_at
            in_col = lax.broadcasted_iota(jnp.int32, (cols, size), 0) == x_at
            in_col = jnp.where(in_col, 1.0, 0.0).astype(jnp.bfloat16)
            amounts = rec_trace_ref[pl.ds(first, share), at : at + size]
            high = amounts.astype(jnp.bfloat16).astype(f32)
            parts = []
            for part in (high, amounts - high):
                for tick in range(share):
                    parts.append(jnp.where(in_row, part[tick : tick + 1], 0.0).astype(jnp.bfloat16))
            total = total + lax.dot_general(
                jnp.concatenate(parts, axis=0),
                in_col,
                (((1,), (1,)), ((), ())),
                preferred_element_type=f32,
            )
        return total

    chunks = -(-count // chunk)
    stops = [min(count, chunk * (-(-chunks * (hop + 1) // bands))) for hop in range(bands)]
    added = add_receivers(jnp.zeros((2 * share * full_y, cols), f32), 0, stops[0])
    for hop in range(1, bands):
        for side in range(2):
            slot = lax.rem(band + hop, bands) * roles + 2 * column + side
            landed(slot)
            for step in range(1, columns):
                pass_on(step, blocks.at[slot], slot, (2 * hop + side) * columns + step)
        added = add_receivers(added, stops[hop - 1], stops[hop])
    size = share * full_y
    high, low = split_two(added[0:size] + added[size : 2 * size])
    lend_ref[0] = high.reshape(share, full_y, cols)
    lend_ref[1] = low.reshape(share, full_y, cols)

    def lend_copy(part):
        return pltpu.make_async_remote_copy(
            src_ref=lend_ref.at[part],
            dst_ref=inject_ref.at[pl.ds(share, share), pl.ds(part * half, full_y)],
            send_sem=lend_send.at[part],
            recv_sem=lend_recv.at[part],
            device_id=partner,
            device_id_type=MESH,
        )

    @pl.when(core == 0)
    def _():
        for part in range(2):
            lend_copy(part).start()

    @pl.when(core == 1)
    def _():
        for part in range(2):
            inject_ref[0:share, part * half : part * half + full_y] = lend_ref[part]

    def table(values):
        found = jnp.zeros(values.shape, f32)
        for level in range(courant_ref.shape[0]):
            found = jnp.where(values == float(level), courant_ref[level], found)
        return found

    def unpack(at_band, at_role, block):
        now = block[0:cells].reshape(depth, rows, cols)
        prev = now - block[cells : 2 * cells].reshape(depth, rows, cols)
        z_part = pl.ds(HALO + depth * at_role, depth)
        y_part = pl.ds(pl.multiple_of(y0 + rows * at_band, rows), rows)
        field_a[z_part, y_part, :] = now
        field_b[z_part, y_part, :] = prev
        speed_ref[pl.ds(depth * at_role, depth), pl.ds(pl.multiple_of(rows * at_band, rows), rows), :] = table(
            block[2 * cells : 3 * cells]
        ).reshape(depth, rows, cols)

    for hop in range(bands):
        for side in range(2):
            at_band, at_role = lax.rem(band + hop, bands), 2 * column + lax.rem(core + side, 2)
            if hop == 0 and side == 0:
                unpack(band, role, out_buf[core].astype(f32))
            else:
                unpack(at_band, at_role, blocks[at_band * roles + at_role].astype(f32))
    for hop in range(bands):
        for step in range(1, columns):
            for side in range(2):
                at_band = lax.rem(band + hop, bands)
                at_role = 2 * lax.rem(column + step, columns) + lax.rem(core + side, 2)
                landed(at_band * roles + at_role)
                unpack(at_band, at_role, blocks[at_band * roles + at_role].astype(f32))

    own_z = pl.ds(HALO + depth * role, depth)
    own_y = pl.ds(pl.multiple_of(y0 + rows * band, rows), rows)
    field_a[own_z, own_y, :] = jnp.where(core == 0, src_now_ref[...], rec_now_ref[...])
    field_b[own_z, own_y, :] = jnp.where(core == 0, src_prev_ref[...], rec_prev_ref[...])

    def store_split(strip, z_at, value):
        high, low = split_two(value)
        line = pl.ds((strip * full_z + z_at) * STRIP, STRIP)
        split_ref[line, 0:cols] = low
        split_ref[line, cols : 2 * cols] = high

    for strip in range(full_y // STRIP):
        for z_at in range(full_z):
            at = y0 + strip * STRIP
            store_split(strip, z_at, field_a[HALO + z_at, at : at + STRIP, :])

    def advance(tick, state, older):
        weights = jnp.concatenate([base_ref[2 * cols : 3 * cols], inject_ref[tick]], axis=0)
        for strip in range(full_y // STRIP):
            at = y0 + strip * STRIP
            part = pl.ds(strip * full_z * STRIP, full_z * STRIP)
            inline = jnp.dot(
                split_ref[part, 0 : 2 * cols], base_ref[0 : 2 * cols], preferred_element_type=f32
            ) + jnp.dot(split_ref[part, cols : 3 * cols], weights, preferred_element_type=f32)
            layers = [state[HALO + z_at, at : at + STRIP, :] for z_at in range(full_z)]
            for z_at in range(full_z):
                total = inline[z_at * STRIP : (z_at + 1) * STRIP]
                z_in = HALO + z_at
                for distance in range(1, 5):
                    pairs = (
                        state[z_in, at - distance : at - distance + STRIP, :]
                        + state[z_in, at + distance : at + distance + STRIP, :]
                    )
                    for other in (z_at - distance, z_at + distance):
                        if 0 <= other < full_z:
                            pairs = pairs + layers[other]
                    total = total + STENCIL_WEIGHTS[distance] * pairs
                updated = (2.0 * layers[z_at] - older[z_in, at : at + STRIP, :]) + (
                    speed_ref[z_at, strip * STRIP : (strip + 1) * STRIP] * total
                )
                older[z_in, at : at + STRIP, :] = updated
                store_split(strip, z_at, updated)

    partner_role = 2 * column + 1 - core
    deep = depth + 2

    def snap_copy(snapshot):
        return pltpu.make_async_remote_copy(
            src_ref=stage_ref.at[snapshot],
            dst_ref=snap_ref.at[snapshot, core],
            send_sem=snap_send.at[snapshot],
            recv_sem=snap_recv.at[snapshot],
            device_id=partner,
            device_id_type=MESH,
        )

    def one_image(snapshot, carry):
        @pl.when((snapshot == IMAGES // 2) & (core == 1))
        def _():
            for part in range(2):
                lend_copy(part).wait_recv()

        for pair in range(SUB // 2):
            advance(SUB * snapshot + 2 * pair, field_a, field_b)
            advance(SUB * snapshot + 2 * pair + 1, field_b, field_a)
        stage_ref[snapshot] = field_a[pl.ds(HALO - 1 + depth * partner_role, deep), own_y, :]
        snap_copy(snapshot).start()
        snap_ref[snapshot, core] = field_a[pl.ds(HALO - 1 + depth * role, deep), own_y, :]
        return carry

    lax.fori_loop(0, IMAGES, one_image, 0)
    def correlate(slot, snapshots, summed):
        lag = lags_ref[slot]
        back = jnp.where(lag > 0, cols - 2 * lag, -2 * lag)
        for snapshot in snapshots:
            moved = pltpu.roll(snap_ref[snapshot, 1].reshape(deep * rows, cols), back, 1)
            summed = summed + snap_ref[snapshot, 0].reshape(deep * rows, cols) * moved
        return summed

    lag_count = lags_ref.shape[0]
    group = -(-lag_count // 4)
    last = IMAGES - 1
    for snapshot in range(last):
        snap_copy(snapshot).wait()

    def early_lag(slot, carry):
        early_ref[slot] = correlate(slot, range(last), jnp.zeros((deep * rows, cols), f32))
        return carry

    lax.fori_loop(0, lag_count, early_lag, 0, unroll=group)
    snap_copy(last).wait()
    results = [
        pltpu.make_async_copy(snap_ref.at[IMAGES - 1, side, pl.ds(1, depth)], kept, out_sem.at[side])
        for side, kept in enumerate((src_out_ref, rec_out_ref))
    ]
    for result in results:
        result.start()

    def one_lag(slot, carry):
        lag = lags_ref[slot]
        shift = jnp.where(lag < 0, cols + lag, lag)
        summed = correlate(slot, (last,), early_ref[slot])
        filtered = (
            2.0 * summed[rows : rows + cells] - summed[0:cells] - summed[2 * rows : 2 * rows + cells]
        )
        filtered = pltpu.roll(filtered, shift, 1)
        lane = lax.broadcasted_iota(jnp.int32, (cells, cols), 1)
        reach = jnp.abs(lag)
        inside = (lane >= reach) & (lane < cols - reach)
        at = pl.multiple_of(slot * cells, cells)
        image_buf[pl.ds(at, cells)] = jnp.where(inside, filtered, 0.0).astype(jnp.bfloat16)
        return carry

    for turn, start in enumerate(range(0, lag_count, group)):
        stop = min(start + group, lag_count)
        lax.fori_loop(start, stop, one_lag, 0, unroll=group)
        part = pl.ds(start * cells, (stop - start) * cells)
        result = pltpu.make_async_copy(image_buf.at[part], image_ref.at[part], out_sem.at[2 + turn])
        result.start()
        results.append(result)
    for result in results:
        result.wait()
    @pl.when(core == 0)
    def _():
        for part in range(2):
            lend_copy(part).wait_send()

    for copy in sends:
        copy.wait_send()


def hand_over(*refs):
    given, kept, held = refs[:3], refs[3:6], refs[6:9]
    first, last = refs[9:]
    arrive = [pltpu.make_async_copy(given[at], held[at], first.at[at]) for at in range(3)]
    leave = [pltpu.make_async_copy(held[at], kept[at], last.at[at]) for at in range(3)]
    for copy in arrive:
        copy.start()
    for at in (1, 2, 0):
        arrive[at].wait()
        leave[at].start()
    for copy in leave:
        copy.wait()


def window_shards(bands, roles, *arrays):
    rec_pos, rec_traces, offset_lags = arrays[8:]
    depth, rows, cols = arrays[0].shape
    cells = depth * rows
    full_z, full_y = depth * roles, rows * bands
    lag_count = offset_lags.shape[0]
    columns = roles // 2
    steps = SUB * IMAGES
    f32, bf16 = jnp.float32, jnp.bfloat16
    hbm = pl.BlockSpec(memory_space=pltpu.HBM)
    arrays = arrays[:8] + (rec_pos.T, rec_traces.T, offset_lags)
    places = [pltpu.SMEM if at in (1, 6, 7, 10) else pltpu.VMEM for at in range(len(arrays))]
    padded = (full_z + 2 * HALO, full_y + 16, cols)
    results = pl.pallas_call(
        functools.partial(window_kernel, bands, roles),
        out_shape=(
            jax.ShapeDtypeStruct((lag_count * cells, cols), bf16),
            jax.ShapeDtypeStruct((depth, rows, cols), f32),
            jax.ShapeDtypeStruct((depth, rows, cols), f32),
        ),
        in_specs=[hbm] * len(arrays),
        out_specs=(hbm, hbm, hbm),
        scratch_shapes=[place(array.shape, array.dtype) for place, array in zip(places, arrays)]
        + [
            pltpu.VMEM((2, 3 * cells, cols), WIRE),
            pltpu.VMEM((bands * roles, 3 * cells, cols), WIRE),
            pltpu.VMEM(padded, f32),
            pltpu.VMEM(padded, f32),
            pltpu.VMEM((full_z, full_y, cols), f32),
            pltpu.VMEM((full_z * full_y, 3 * cols), bf16),
            pltpu.VMEM((3 * cols, cols), bf16),
            pltpu.VMEM((steps, cols, cols), bf16),
            pltpu.VMEM((IMAGES, depth + 2, rows, cols), f32),
            pltpu.VMEM((IMAGES, 2, depth + 2, rows, cols), f32),
            pltpu.SemaphoreType.DMA((2 * bands,)),
            pltpu.SemaphoreType.DMA((2 * bands * columns,)),
            pltpu.SemaphoreType.DMA((bands * roles,)),
            pltpu.SemaphoreType.DMA((IMAGES,)),
            pltpu.SemaphoreType.DMA((IMAGES,)),
            pltpu.VMEM((2, steps // 2, full_y, cols), bf16),
            pltpu.VMEM((lag_count * cells, cols), bf16),
            pltpu.VMEM((lag_count, cells + 2 * rows, cols), f32),
            pltpu.SemaphoreType.DMA((6,)),
            pltpu.SemaphoreType.DMA((len(arrays),)),
            pltpu.SemaphoreType.DMA((2,)),
            pltpu.SemaphoreType.DMA((2,)),
        ],
        compiler_params=pltpu.CompilerParams(
            collective_id=0, has_side_effects=True, vmem_limit_bytes=VMEM_GRANT
        ),
    )(*arrays)
    image, source, receiver = pl.pallas_call(
        hand_over,
        out_shape=tuple(jax.ShapeDtypeStruct(result.shape, result.dtype) for result in results),
        in_specs=[hbm] * 3,
        out_specs=(hbm, hbm, hbm),
        scratch_shapes=[pltpu.VMEM(result.shape, result.dtype) for result in results]
        + [pltpu.SemaphoreType.DMA((3,)), pltpu.SemaphoreType.DMA((3,))],
        compiler_params=pltpu.CompilerParams(vmem_limit_bytes=VMEM_GRANT),
    )(*results)
    return image.reshape(lag_count, depth, rows, cols), source, receiver


def shards(bands, roles, *arrays):
    depth, rows, cols = arrays[0].shape
    sources = arrays[6].shape[0]
    small = depth * roles * rows * bands * cols <= WINDOW_CELLS
    fits = roles % 2 == 0 and rows % 8 == 0 and cols % 128 == 0
    fits = fits and max(rows * bands, sources) <= cols // 2 and arrays[10].shape[0] < cols
    fits = fits and (depth * rows) % 16 == 0 and (rows * bands) % STRIP == 0 and arrays[1].shape[0] <= 256
    if small and fits:
        return window_shards(bands, roles, *arrays)
    return tile_shards(*arrays)


def solution(mesh):
    placed = (
        P("role", "band", None),
        P(),
        P(("survey", "role"), "band", None),
        P(("survey", "role"), "band", None),
        P(("survey", "role"), "band", None),
        P(("survey", "role"), "band", None),
        P("survey", None),
        P("survey", None),
        P("survey", None),
        P("survey", None),
        P(),
    )
    return jax.shard_map(
        functools.partial(shards, mesh.shape["band"], mesh.shape["role"]),
        mesh=mesh,
        in_specs=placed,
        out_specs=(
            P("survey", "role", "band", None),
            P(("survey", "role"), "band", None),
            P(("survey", "role"), "band", None),
        ),
        check_vma=False,
    )
```

```python
import functools

import jax
import jax.numpy as jnp
from jax import lax
from jax.experimental import pallas as pl
from jax.experimental.pallas import tpu as pltpu
from jax.sharding import PartitionSpec as P

SUB = 4
IMAGES = 4
HALO = 4
WINDOW_CELLS = 1 << 17
MESH = pl.DeviceIdType.MESH
STRIP = 16
WIRE = jnp.bfloat16
VMEM_GRANT = 64 * 1024 * 1024


STENCIL_WEIGHTS = (-205.0 / 72.0, 8.0 / 5.0, -1.0 / 5.0, 8.0 / 315.0, -1.0 / 560.0)


def padded_2(block, sides, width):
    for axis, dim in sides:
        count = lax.axis_size(axis)
        forward = [(i, i + 1) for i in range(count - 1)]
        backward = [(target, source) for source, target in forward]
        low = lax.ppermute(
            lax.slice_in_dim(block, block.shape[dim] - width, None, axis=dim), axis, forward
        )
        high = lax.ppermute(lax.slice_in_dim(block, 0, width, axis=dim), axis, backward)
        block = jnp.concatenate([low, block, high], axis=dim)
    return block


def laplace(padded, depth_cells, row_cells, col_cells):

    def window(along_z, along_y, along_x):
        return padded[
            :,
            4 + along_z : 4 + along_z + depth_cells,
            4 + along_y : 4 + along_y + row_cells,
            4 + along_x : 4 + along_x + col_cells,
        ]

    summed = 3.0 * STENCIL_WEIGHTS[0] * window(0, 0, 0)
    for distance in range(1, 5):
        weight = STENCIL_WEIGHTS[distance]
        pairs = window(distance, 0, 0) + window(-distance, 0, 0)
        pairs = pairs + window(0, distance, 0) + window(0, -distance, 0)
        pairs = pairs + window(0, 0, distance) + window(0, 0, -distance)
        summed = summed + weight * pairs
    return summed


def lookup(vel_index, courant):
    levels = courant.shape[0]

    def add_level(level, summed):
        return summed + jnp.where(vel_index == level, courant[level], 0.0)

    return lax.fori_loop(0, levels, add_level, jnp.zeros(vel_index.shape, jnp.float32))


def local_index(global_at, start, extent):
    local_at = global_at - start
    inside = (local_at >= 0) & (local_at < extent)
    return jnp.where(inside, local_at, extent)


def inject_all(shape, depth_at, row_at, col_at, amounts):
    step_count = amounts.shape[1]
    return (
        jnp.zeros((step_count,) + shape, jnp.float32)
        .at[:, depth_at, row_at, col_at]
        .add(amounts.T, mode="drop")
    )


def lag_products(source_pad, receiver_pad, offset_lags, max_lag, col_cells):

    def product(lag_value):
        src_part = lax.dynamic_slice_in_dim(source_pad, max_lag - lag_value, col_cells, 2)
        rec_part = lax.dynamic_slice_in_dim(receiver_pad, max_lag + lag_value, col_cells, 2)
        return src_part * rec_part

    return jax.vmap(product)(offset_lags)


def depth_filter(padded, depth_cells):
    return (
        2.0 * padded[:, 1 : 1 + depth_cells]
        - padded[:, 0:depth_cells]
        - padded[:, 2 : 2 + depth_cells]
    )


def pad_inline(state, max_lag):
    return jnp.pad(state, ((0, 0), (0, 0), (0, 0), (max_lag, max_lag)))


def accumulate(slab_state, image_sum, edge_sum, offset_lags, max_lag):
    col_cells = slab_state.shape[3]
    padded = pad_inline(slab_state, max_lag)
    image_sum = image_sum + lag_products(padded[0], padded[1], offset_lags, max_lag, col_cells)
    return (image_sum, edge_sum)


def finish(image_sum):
    padded = padded_2(image_sum, (("role", 1),), 1)
    return depth_filter(padded, image_sum.shape[1]).astype(jnp.bfloat16)


def tile_shards(
    vel_index,
    courant,
    src_now,
    src_prev,
    rec_now,
    rec_prev,
    src_pos,
    src_wavelet,
    rec_pos,
    rec_traces,
    offset_lags,
):
    lag_count = offset_lags.shape[0]
    max_lag = lag_count // 2
    speed = lookup(vel_index, courant)
    band_start = lax.axis_index("band") * src_now.shape[1]
    role_at = lax.axis_index("role")
    current = jnp.stack([src_now, rec_now])
    previous = jnp.stack([src_prev, rec_prev])
    depth_start = role_at * src_now.shape[0]
    col_start = 0

    def faces(state):
        padded = padded_2(state, (("band", 2), ("role", 1)), 4)
        return jnp.pad(padded, ((0, 0), (0, 0), (0, 0), (4, 4)))

    depth_cells, row_cells, col_cells = speed.shape
    shape = speed.shape
    slab_shape = src_now.shape
    src_depth = local_index(src_pos[:, 0], depth_start, depth_cells)
    src_row = local_index(src_pos[:, 1], band_start, row_cells)
    src_col = local_index(src_pos[:, 2], col_start, col_cells)
    rec_depth = local_index(jnp.zeros_like(rec_pos[:, 0]), depth_start, depth_cells)
    rec_row = local_index(rec_pos[:, 0], band_start, row_cells)
    rec_col = local_index(rec_pos[:, 1], col_start, col_cells)
    src_terms = inject_all(shape, src_depth, src_row, src_col, src_wavelet)
    rec_terms = inject_all(shape, rec_depth, rec_row, rec_col, rec_traces)
    image_sum = jnp.zeros((lag_count,) + slab_shape, jnp.float32)
    edge_sum = jnp.zeros((lag_count, 2) + slab_shape[1:], jnp.float32)
    slab_state = current
    for snapshot in range(IMAGES):

        def advance(substep, carry):
            state, older = carry
            tick_at = snapshot * SUB + substep
            sources = jnp.stack(
                [
                    lax.dynamic_index_in_dim(src_terms, tick_at, 0, keepdims=False),
                    lax.dynamic_index_in_dim(rec_terms, tick_at, 0, keepdims=False),
                ]
            )
            laplacian = laplace(faces(state), depth_cells, row_cells, col_cells)
            updated = 2.0 * state - older + speed * (laplacian + sources)
            return (updated, state)

        current, previous = lax.fori_loop(0, SUB, advance, (current, previous))
        slab_state = current
        image_sum, edge_sum = accumulate(slab_state, image_sum, edge_sum, offset_lags, max_lag)
    image = finish(image_sum)
    return (image, slab_state[0], slab_state[1])


def split_two(value):
    high = value.astype(jnp.bfloat16)
    low = (value - high.astype(jnp.float32)).astype(jnp.bfloat16)
    return high, low


def inline_matrix(cols):
    row = lax.broadcasted_iota(jnp.int32, (cols, cols), 0)
    col = lax.broadcasted_iota(jnp.int32, (cols, cols), 1)
    apart = jnp.abs(row - col)
    matrix = jnp.where(apart == 0, 3.0 * STENCIL_WEIGHTS[0], 0.0)
    for distance in range(1, 5):
        matrix = jnp.where(apart == distance, STENCIL_WEIGHTS[distance], matrix)
    return matrix


def window_kernel(
    bands,
    roles,
    *refs,
):
    inputs, outputs, held = refs[:11], refs[11:14], refs[14:25]
    (
        vel_ref,
        courant_ref,
        src_now_ref,
        src_prev_ref,
        rec_now_ref,
        rec_prev_ref,
        src_pos_ref,
        src_wave_ref,
        rec_pos_ref,
        rec_trace_ref,
        lags_ref,
    ) = held
    image_ref, src_out_ref, rec_out_ref = outputs
    (
        out_buf,
        blocks,
        field_a,
        field_b,
        speed_ref,
        split_ref,
        base_ref,
        inject_ref,
        stage_ref,
        snap_ref,
        near_send,
        far_send,
        block_recv,
        snap_send,
        snap_recv,
        lend_ref,
        image_buf,
        early_ref,
        out_sem,
        in_sem,
        lend_send,
        lend_recv,
    ) = refs[25:]
    fetches = [
        pltpu.make_async_copy(given, kept, in_sem.at[at])
        for at, (given, kept) in enumerate(zip(inputs, held))
    ]
    for fetch in fetches:
        fetch.start()
    inject_ref[...] = jnp.zeros_like(inject_ref)
    depth, rows, cols = vel_ref.shape
    full_z, full_y = depth * roles, rows * bands
    cells = depth * rows
    columns = roles // 2
    survey = lax.axis_index("survey")
    band = lax.axis_index("band")
    role = lax.axis_index("role")
    core = lax.rem(role, 2)
    column = role // 2
    own = band * roles + role
    f32 = jnp.float32
    y0 = 8

    def device(at_band, at_role):
        return (survey, at_band, at_role)

    partner = device(band, 2 * column + 1 - core)
    barrier = pltpu.get_barrier_semaphore()
    greeted = 0
    for step in range(1, bands):
        for side in range(2):
            pl.semaphore_signal(
                barrier,
                inc=1,
                device_id=device(lax.rem(band + step, bands), 2 * column + side),
                device_id_type=MESH,
            )
            greeted += 1
    pl.semaphore_signal(barrier, inc=1, device_id=partner, device_id_type=MESH)
    greeted += 1
    for step in range(1, columns):
        pl.semaphore_signal(
            barrier,
            inc=1,
            device_id=device(band, 2 * lax.rem(column + step, columns) + core),
            device_id_type=MESH,
        )
        greeted += 1

    for at in (0, 2, 3, 4, 5):
        fetches[at].wait()
    index = vel_ref[...].astype(f32).reshape(cells, cols)
    for side, now_ref, prev_ref in ((0, src_now_ref, src_prev_ref), (1, rec_now_ref, rec_prev_ref)):
        now = now_ref[...].reshape(cells, cols)
        change = now - prev_ref[...].reshape(cells, cols)
        out_buf[side, 0:cells] = now.astype(WIRE)
        out_buf[side, cells : 2 * cells] = change.astype(WIRE)
        out_buf[side, 2 * cells : 3 * cells] = index.astype(WIRE)
    pl.semaphore_wait(barrier, greeted)

    sends = []
    for step in range(1, bands):
        for side in range(2):
            copy = pltpu.make_async_remote_copy(
                src_ref=out_buf.at[side],
                dst_ref=blocks.at[own],
                send_sem=near_send.at[2 * step + side],
                recv_sem=block_recv.at[own],
                device_id=device(lax.rem(band + step, bands), 2 * column + side),
                device_id_type=MESH,
            )
            copy.start()
            sends.append(copy)
    copy = pltpu.make_async_remote_copy(
        src_ref=out_buf.at[1 - core],
        dst_ref=blocks.at[own],
        send_sem=near_send.at[0],
        recv_sem=block_recv.at[own],
        device_id=partner,
        device_id_type=MESH,
    )
    copy.start()
    sends.append(copy)

    def pass_on(step, source, slot, lane):
        copy = pltpu.make_async_remote_copy(
            src_ref=source,
            dst_ref=blocks.at[slot],
            send_sem=far_send.at[lane],
            recv_sem=block_recv.at[slot],
            device_id=device(band, 2 * lax.rem(column + step, columns) + core),
            device_id_type=MESH,
        )
        copy.start()
        sends.append(copy)

    def landed(slot):
        pltpu.make_async_copy(blocks.at[slot], blocks.at[slot], block_recv.at[slot]).wait()

    for step in range(1, columns):
        pass_on(step, out_buf.at[core], own, step)

    high, low = split_two(inline_matrix(cols))
    base_ref[0:cols] = high
    base_ref[cols : 2 * cols] = high
    base_ref[2 * cols : 3 * cols] = low
    field_a[...] = jnp.zeros_like(field_a)
    field_b[...] = jnp.zeros_like(field_b)

    slot = band * roles + 2 * column + 1 - core
    landed(slot)
    for step in range(1, columns):
        pass_on(step, blocks.at[slot], slot, columns + step)

    for at in (1, 6, 7, 8, 9, 10):
        fetches[at].wait()
    lines = split_ref.shape[0]
    half = cols // 2
    row_at = lax.broadcasted_iota(jnp.int32, (lines, cols), 0)
    lane_at = lax.broadcasted_iota(jnp.int32, (lines, cols), 1)
    lane_low = jnp.where(lane_at >= half, lane_at - half, lane_at)
    steps = inject_ref.shape[0]

    @pl.when(core == 0)
    def _():
        count = src_pos_ref.shape[0]
        target = jnp.full((1, cols), -1, jnp.int32)
        lane = lax.broadcasted_iota(jnp.int32, (1, cols), 1)
        lane = jnp.where(lane >= half, lane - half, lane)
        for source in range(count):
            y_at = src_pos_ref[source, 1]
            strip = lax.div(y_at, STRIP)
            line = (strip * full_z + src_pos_ref[source, 0]) * STRIP + y_at - strip * STRIP
            target = jnp.where(lane == source, line, target)
        split_ref[:, 2 * cols : 3 * cols] = jnp.where(row_at == target, 1.0, 0.0).astype(jnp.bfloat16)
        height = -(-count // 16) * 16
        row = lax.broadcasted_iota(jnp.int32, (height, cols), 0)
        col = lax.broadcasted_iota(jnp.int32, (height, cols), 1)
        for tick in range(steps):
            term = jnp.zeros((height, cols), f32)
            for source in range(count):
                here = (row == source) & (col == src_pos_ref[source, 2])
                term = jnp.where(here, src_wave_ref[source, tick], term)
            high, low = split_two(term)
            inject_ref[tick, 0:height] = high
            inject_ref[tick, half : half + height] = low

    @pl.when(core == 1)
    def _():
        split_ref[:, 2 * cols : 3 * cols] = jnp.zeros((lines, cols), jnp.bfloat16)
        for strip in range(full_y // STRIP):
            same = row_at[0:STRIP] + strip * STRIP == lane_low[0:STRIP]
            top = pl.ds(strip * full_z * STRIP, STRIP)
            split_ref[top, 2 * cols : 3 * cols] = jnp.where(same, 1.0, 0.0).astype(jnp.bfloat16)

    share = steps // 2
    first = pl.multiple_of(share * (1 - core), share)
    count = rec_pos_ref.shape[1]
    chunk = min(512, count)

    def add_receivers(total, start, stop):
        for at in range(start, stop, chunk):
            size = min(chunk, stop - at)
            y_at = rec_pos_ref[0:1, at : at + size]
            x_at = rec_pos_ref[1:2, at : at + size]
            in_row = lax.broadcasted_iota(jnp.int32, (full_y, size), 0) == y_at
            in_col = lax.broadcasted_iota(jnp.int32, (cols, size), 0) == x_at
            in_col = jnp.where(in_col, 1.0, 0.0).astype(jnp.bfloat16)
            amounts = rec_trace_ref[pl.ds(first, share), at : at + size]
            high = amounts.astype(jnp.bfloat16).astype(f32)
            masks = [
                jnp.where(in_row[at_row : at_row + STRIP], 1.0, 0.0).astype(jnp.bfloat16)
                for at_row in range(0, full_y, STRIP)
            ]
            parts = []
            for part in (high, amounts - high):
                for tick in range(share):
                    line = jnp.broadcast_to(part[tick : tick + 1], (STRIP, size)).astype(jnp.bfloat16)
                    parts.extend(mask * line for mask in masks)
            total = total + lax.dot_general(
                jnp.concatenate(parts, axis=0),
                in_col,
                (((1,), (1,)), ((), ())),
                preferred_element_type=f32,
            )
        return total

    chunks = -(-count // chunk)
    stops = [min(count, chunk * (-(-chunks * (hop + 1) // bands))) for hop in range(bands)]
    added = add_receivers(jnp.zeros((2 * share * full_y, cols), f32), 0, stops[0])
    for hop in range(1, bands):
        for side in range(2):
            slot = lax.rem(band + hop, bands) * roles + 2 * column + side
            landed(slot)
            for step in range(1, columns):
                pass_on(step, blocks.at[slot], slot, (2 * hop + side) * columns + step)
        added = add_receivers(added, stops[hop - 1], stops[hop])
    size = share * full_y
    high, low = split_two(added[0:size] + added[size : 2 * size])
    lend_ref[0] = high.reshape(share, full_y, cols)
    lend_ref[1] = low.reshape(share, full_y, cols)

    def lend_copy(part):
        return pltpu.make_async_remote_copy(
            src_ref=lend_ref.at[part],
            dst_ref=inject_ref.at[pl.ds(share, share), pl.ds(part * half, full_y)],
            send_sem=lend_send.at[part],
            recv_sem=lend_recv.at[part],
            device_id=partner,
            device_id_type=MESH,
        )

    @pl.when(core == 0)
    def _():
        for part in range(2):
            lend_copy(part).start()

    @pl.when(core == 1)
    def _():
        for part in range(2):
            inject_ref[0:share, part * half : part * half + full_y] = lend_ref[part]

    def table(values):
        found = jnp.zeros(values.shape, f32)
        for level in range(courant_ref.shape[0]):
            found = jnp.where(values == float(level), courant_ref[level], found)
        return found

    def unpack(at_band, at_role, block):
        now = block[0:cells].reshape(depth, rows, cols)
        prev = now - block[cells : 2 * cells].reshape(depth, rows, cols)
        z_part = pl.ds(HALO + depth * at_role, depth)
        y_part = pl.ds(pl.multiple_of(y0 + rows * at_band, rows), rows)
        field_a[z_part, y_part, :] = now
        field_b[z_part, y_part, :] = prev
        speed_ref[pl.ds(depth * at_role, depth), pl.ds(pl.multiple_of(rows * at_band, rows), rows), :] = table(
            block[2 * cells : 3 * cells]
        ).reshape(depth, rows, cols)

    for hop in range(bands):
        for side in range(2):
            at_band, at_role = lax.rem(band + hop, bands), 2 * column + lax.rem(core + side, 2)
            if hop == 0 and side == 0:
                unpack(band, role, out_buf[core].astype(f32))
            else:
                unpack(at_band, at_role, blocks[at_band * roles + at_role].astype(f32))
    for hop in range(bands):
        for step in range(1, columns):
            for side in range(2):
                at_band = lax.rem(band + hop, bands)
                at_role = 2 * lax.rem(column + step, columns) + lax.rem(core + side, 2)
                landed(at_band * roles + at_role)
                unpack(at_band, at_role, blocks[at_band * roles + at_role].astype(f32))

    own_z = pl.ds(HALO + depth * role, depth)
    own_y = pl.ds(pl.multiple_of(y0 + rows * band, rows), rows)
    field_a[own_z, own_y, :] = jnp.where(core == 0, src_now_ref[...], rec_now_ref[...])
    field_b[own_z, own_y, :] = jnp.where(core == 0, src_prev_ref[...], rec_prev_ref[...])

    def store_split(strip, z_at, value):
        high, low = split_two(value)
        line = pl.ds((strip * full_z + z_at) * STRIP, STRIP)
        split_ref[line, 0:cols] = low
        split_ref[line, cols : 2 * cols] = high

    for strip in range(full_y // STRIP):
        for z_at in range(full_z):
            at = y0 + strip * STRIP
            store_split(strip, z_at, field_a[HALO + z_at, at : at + STRIP, :])

    def advance(tick, state, older):
        weights = jnp.concatenate([base_ref[2 * cols : 3 * cols], inject_ref[tick]], axis=0)
        for strip in range(full_y // STRIP):
            at = y0 + strip * STRIP
            part = pl.ds(strip * full_z * STRIP, full_z * STRIP)
            inline = jnp.dot(
                split_ref[part, 0 : 2 * cols], base_ref[0 : 2 * cols], preferred_element_type=f32
            ) + jnp.dot(split_ref[part, cols : 3 * cols], weights, preferred_element_type=f32)
            layers = [state[HALO + z_at, at : at + STRIP, :] for z_at in range(full_z)]
            for z_at in range(full_z):
                total = inline[z_at * STRIP : (z_at + 1) * STRIP]
                z_in = HALO + z_at
                for distance in range(1, 5):
                    pairs = (
                        state[z_in, at - distance : at - distance + STRIP, :]
                        + state[z_in, at + distance : at + distance + STRIP, :]
                    )
                    for other in (z_at - distance, z_at + distance):
                        if 0 <= other < full_z:
                            pairs = pairs + layers[other]
                    total = total + STENCIL_WEIGHTS[distance] * pairs
                updated = (2.0 * layers[z_at] - older[z_in, at : at + STRIP, :]) + (
                    speed_ref[z_at, strip * STRIP : (strip + 1) * STRIP] * total
                )
                older[z_in, at : at + STRIP, :] = updated
                store_split(strip, z_at, updated)

    partner_role = 2 * column + 1 - core
    deep = depth + 2

    def snap_copy(snapshot):
        return pltpu.make_async_remote_copy(
            src_ref=stage_ref.at[snapshot],
            dst_ref=snap_ref.at[snapshot, core],
            send_sem=snap_send.at[snapshot],
            recv_sem=snap_recv.at[snapshot],
            device_id=partner,
            device_id_type=MESH,
        )

    def one_image(snapshot, carry):
        @pl.when((snapshot == IMAGES // 2) & (core == 1))
        def _():
            for part in range(2):
                lend_copy(part).wait_recv()

        for pair in range(SUB // 2):
            advance(SUB * snapshot + 2 * pair, field_a, field_b)
            advance(SUB * snapshot + 2 * pair + 1, field_b, field_a)
        stage_ref[snapshot] = field_a[pl.ds(HALO - 1 + depth * partner_role, deep), own_y, :]
        snap_copy(snapshot).start()
        snap_ref[snapshot, core] = field_a[pl.ds(HALO - 1 + depth * role, deep), own_y, :]
        return carry

    lax.fori_loop(0, IMAGES, one_image, 0)
    def correlate(slot, snapshots, summed):
        lag = lags_ref[slot]
        back = jnp.where(lag > 0, cols - 2 * lag, -2 * lag)
        for snapshot in snapshots:
            moved = pltpu.roll(snap_ref[snapshot, 1].reshape(deep * rows, cols), back, 1)
            summed = summed + snap_ref[snapshot, 0].reshape(deep * rows, cols) * moved
        return summed

    lag_count = lags_ref.shape[0]
    group = -(-lag_count // 4)
    last = IMAGES - 1
    for snapshot in range(last):
        snap_copy(snapshot).wait()

    def early_lag(slot, carry):
        early_ref[slot] = correlate(slot, range(last), jnp.zeros((deep * rows, cols), f32))
        return carry

    lax.fori_loop(0, lag_count, early_lag, 0, unroll=group)
    snap_copy(last).wait()
    results = [
        pltpu.make_async_copy(snap_ref.at[IMAGES - 1, side, pl.ds(1, depth)], kept, out_sem.at[side])
        for side, kept in enumerate((src_out_ref, rec_out_ref))
    ]
    for result in results:
        result.start()

    def one_lag(slot, carry):
        lag = lags_ref[slot]
        shift = jnp.where(lag < 0, cols + lag, lag)
        summed = correlate(slot, (last,), early_ref[slot])
        filtered = (
            2.0 * summed[rows : rows + cells] - summed[0:cells] - summed[2 * rows : 2 * rows + cells]
        )
        filtered = pltpu.roll(filtered, shift, 1)
        lane = lax.broadcasted_iota(jnp.int32, (cells, cols), 1)
        reach = jnp.abs(lag)
        inside = (lane >= reach) & (lane < cols - reach)
        at = pl.multiple_of(slot * cells, cells)
        image_buf[pl.ds(at, cells)] = jnp.where(inside, filtered, 0.0).astype(jnp.bfloat16)
        return carry

    for turn, start in enumerate(range(0, lag_count, group)):
        stop = min(start + group, lag_count)
        lax.fori_loop(start, stop, one_lag, 0, unroll=group)
        part = pl.ds(start * cells, (stop - start) * cells)
        result = pltpu.make_async_copy(image_buf.at[part], image_ref.at[part], out_sem.at[2 + turn])
        result.start()
        results.append(result)
    for result in results:
        result.wait()
    @pl.when(core == 0)
    def _():
        for part in range(2):
            lend_copy(part).wait_send()

    for copy in sends:
        copy.wait_send()


def hand_over(*refs):
    given, kept, held = refs[:3], refs[3:6], refs[6:9]
    first, last = refs[9:]
    arrive = [pltpu.make_async_copy(given[at], held[at], first.at[at]) for at in range(3)]
    leave = [pltpu.make_async_copy(held[at], kept[at], last.at[at]) for at in range(3)]
    for copy in arrive:
        copy.start()
    for at in (1, 2, 0):
        arrive[at].wait()
        leave[at].start()
    for copy in leave:
        copy.wait()


def window_shards(bands, roles, *arrays):
    rec_pos, rec_traces, offset_lags = arrays[8:]
    depth, rows, cols = arrays[0].shape
    cells = depth * rows
    full_z, full_y = depth * roles, rows * bands
    lag_count = offset_lags.shape[0]
    columns = roles // 2
    steps = SUB * IMAGES
    f32, bf16 = jnp.float32, jnp.bfloat16
    hbm = pl.BlockSpec(memory_space=pltpu.HBM)
    arrays = arrays[:8] + (rec_pos.T, rec_traces.T, offset_lags)
    places = [pltpu.SMEM if at in (1, 6, 7, 10) else pltpu.VMEM for at in range(len(arrays))]
    padded = (full_z + 2 * HALO, full_y + 16, cols)
    results = pl.pallas_call(
        functools.partial(window_kernel, bands, roles),
        out_shape=(
            jax.ShapeDtypeStruct((lag_count * cells, cols), bf16),
            jax.ShapeDtypeStruct((depth, rows, cols), f32),
            jax.ShapeDtypeStruct((depth, rows, cols), f32),
        ),
        in_specs=[hbm] * len(arrays),
        out_specs=(hbm, hbm, hbm),
        scratch_shapes=[place(array.shape, array.dtype) for place, array in zip(places, arrays)]
        + [
            pltpu.VMEM((2, 3 * cells, cols), WIRE),
            pltpu.VMEM((bands * roles, 3 * cells, cols), WIRE),
            pltpu.VMEM(padded, f32),
            pltpu.VMEM(padded, f32),
            pltpu.VMEM((full_z, full_y, cols), f32),
            pltpu.VMEM((full_z * full_y, 3 * cols), bf16),
            pltpu.VMEM((3 * cols, cols), bf16),
            pltpu.VMEM((steps, cols, cols), bf16),
            pltpu.VMEM((IMAGES, depth + 2, rows, cols), f32),
            pltpu.VMEM((IMAGES, 2, depth + 2, rows, cols), f32),
            pltpu.SemaphoreType.DMA((2 * bands,)),
            pltpu.SemaphoreType.DMA((2 * bands * columns,)),
            pltpu.SemaphoreType.DMA((bands * roles,)),
            pltpu.SemaphoreType.DMA((IMAGES,)),
            pltpu.SemaphoreType.DMA((IMAGES,)),
            pltpu.VMEM((2, steps // 2, full_y, cols), bf16),
            pltpu.VMEM((lag_count * cells, cols), bf16),
            pltpu.VMEM((lag_count, cells + 2 * rows, cols), f32),
            pltpu.SemaphoreType.DMA((6,)),
            pltpu.SemaphoreType.DMA((len(arrays),)),
            pltpu.SemaphoreType.DMA((2,)),
            pltpu.SemaphoreType.DMA((2,)),
        ],
        compiler_params=pltpu.CompilerParams(
            collective_id=0, has_side_effects=True, vmem_limit_bytes=VMEM_GRANT
        ),
    )(*arrays)
    image, source, receiver = pl.pallas_call(
        hand_over,
        out_shape=tuple(jax.ShapeDtypeStruct(result.shape, result.dtype) for result in results),
        in_specs=[hbm] * 3,
        out_specs=(hbm, hbm, hbm),
        scratch_shapes=[pltpu.VMEM(result.shape, result.dtype) for result in results]
        + [pltpu.SemaphoreType.DMA((3,)), pltpu.SemaphoreType.DMA((3,))],
        compiler_params=pltpu.CompilerParams(vmem_limit_bytes=VMEM_GRANT),
    )(*results)
    return image.reshape(lag_count, depth, rows, cols), source, receiver


def shards(bands, roles, *arrays):
    depth, rows, cols = arrays[0].shape
    sources = arrays[6].shape[0]
    small = depth * roles * rows * bands * cols <= WINDOW_CELLS
    fits = roles % 2 == 0 and rows % 8 == 0 and cols % 128 == 0
    fits = fits and max(rows * bands, sources) <= cols // 2 and arrays[10].shape[0] < cols
    fits = fits and (depth * rows) % 16 == 0 and (rows * bands) % STRIP == 0 and arrays[1].shape[0] <= 256
    if small and fits:
        return window_shards(bands, roles, *arrays)
    return tile_shards(*arrays)


def solution(mesh):
    placed = (
        P("role", "band", None),
        P(),
        P(("survey", "role"), "band", None),
        P(("survey", "role"), "band", None),
        P(("survey", "role"), "band", None),
        P(("survey", "role"), "band", None),
        P("survey", None),
        P("survey", None),
        P("survey", None),
        P("survey", None),
        P(),
    )
    return jax.shard_map(
        functools.partial(shards, mesh.shape["band"], mesh.shape["role"]),
        mesh=mesh,
        in_specs=placed,
        out_specs=(
            P("survey", "role", "band", None),
            P(("survey", "role"), "band", None),
            P(("survey", "role"), "band", None),
        ),
        check_vma=False,
    )
```
